32 devices in a mesh: ctx: 8 (over y, x, core), head: 4 (over z).
Axes of the slice: x: 2, y: 2, z: 4, core: 2. Of those that a mesh axis runs over, the one named last changes fastest.
Arguments:
- tokens: bfloat16 [2, 2, 1536, 2560], P(None, None, 'ctx'), may hold values from -6 to 6
- lengths: int32 [2, 2], replicated, may hold values from 1024 to 1536, as said below
- cotangent: bfloat16 [2, 2, 1536, 2560], P(None, None, 'ctx'), may hold values from -6 to 6
- attn_gain: bfloat16 [2560], P('ctx'), may hold values from 0.5 to 1.5
- query_weight: bfloat16 [2560, 2560], P('ctx', 'head'), may hold values from -0.125 to 0.125
- key_weight: bfloat16 [2560, 640], P('ctx', 'head'), may hold values from -0.125 to 0.125
- value_weight: bfloat16 [2560, 640], P('ctx', 'head'), may hold values from -0.125 to 0.125
- out_weight: bfloat16 [2560, 2560], P('head', 'ctx'), may hold values from -1.25 to 1.25
- ffn_gain: bfloat16 [2560], P('ctx'), may hold values from 0.5 to 1.5
- gate_weight: bfloat16 [2560, 6912], P('ctx', 'head'), may hold values from -0.125 to 0.125
- up_weight: bfloat16 [2560, 6912], P('ctx', 'head'), may hold values from -0.125 to 0.125
- down_weight: bfloat16 [6912, 2560], P('head', 'ctx'), may hold values from -0.078125 to 0.078125
Outputs:
- mixed: bfloat16 [2, 2, 1536, 2560], P(None, None, 'ctx')
- token_grad: float32 [2, 2, 1536, 2560], P(None, None, 'ctx')
- attn_gain_grad: float32 [2560], P('ctx')
- query_grad: float32 [2560, 2560], P('ctx', 'head')
- key_grad: float32 [2560, 640], P('ctx', 'head')
- value_grad: float32 [2560, 640], P('ctx', 'head')
- out_grad: float32 [2560, 2560], P('head', 'ctx')
- ffn_gain_grad: float32 [2560], P('ctx')
- gate_grad: float32 [2560, 6912], P('ctx', 'head')
- up_grad: float32 [2560, 6912], P('ctx', 'head')
- down_grad: float32 [6912, 2560], P('head', 'ctx')
The draws below stay inside these ranges and needn't reach their ends.
Inputs may be any that keep to these rules, and one draw needn't show every extreme that they name: `lengths`: in each micro-batch one sequence, chosen by the seed, has all 1536 slots live.
All inputs are finite; a program needn't handle non-finite values.
Results may differ from the reference program's by a relative error of at most 0.022.
Values may be sent and summed in bfloat16 or wider, within the bound.
No kernel may reach another device: no remote copies, remote signals or barrier semaphores. Data moves between devices by JAX's collectives and lax.ppermute only.
A program may use at most 320 MiB of HBM per device.

```python
import jax
import jax.numpy as jnp
from jax import lax

D = 2560
HEADS = 32
KV_HEADS = 8
HD = 80
FF = 6912
WINDOW = 4096
SEQS = 2
MICRO = 2
MIN_LEN = 1024
PAD = 1536


def draw_lengths(key, part):
    key = jax.random.fold_in(key, 7)
    first_key, second_key = jax.random.split(key)
    drawn = jax.random.randint(first_key, (MICRO, SEQS), MIN_LEN, PAD + 1)
    longest = jax.random.randint(second_key, (MICRO,), 0, SEQS)
    chosen = jnp.arange(SEQS)[None, :] == longest[:, None]
    return jnp.where(chosen, PAD, drawn).astype(jnp.int32)


def levels(stream_key, dims, cuts, smallest, high):
    def one(axis_at, parts):
        heights = jax.random.uniform(jax.random.fold_in(jax.random.fold_in(stream_key, 6), axis_at), (parts,), jnp.float32, smallest / len(cuts), high / len(cuts))
        return jnp.repeat(jnp.exp(heights), dims[axis_at] // parts).reshape((-1,) + (1,) * (len(dims) - axis_at - 1))

    level = one(*cuts[0])
    for cut in cuts[1:]:
        level = level * one(*cut)
    return level


def bell_draw(key, dims, width, bound, pieces=(), kind=jnp.bfloat16):
    level = levels(key, dims, pieces, -0.22, 0.18) if pieces else 1.0
    values = jax.random.normal(key, dims, jnp.float32) * width * level
    return jnp.minimum(jnp.maximum(values, -bound), bound).astype(kind)


def setup_inputs(seed: int = 0) -> dict:
    splits = jax.random.split(jax.random.key(seed), 13)
    tokens = bell_draw(splits[0], (MICRO, SEQS, PAD, D), 1.0, 6.0, ((2, 8),))
    lengths = draw_lengths(jax.random.fold_in(splits[12], 71), 0)
    cotangent = bell_draw(splits[2], (MICRO, SEQS, PAD, D), 1.0, 6.0, ((2, 8),))
    attn_gain = jnp.clip(1.0 + 0.1 * jax.random.normal(splits[3], (D,), jnp.float32), 0.5, 1.5).astype(jnp.bfloat16)
    query_weight = bell_draw(splits[4], (D, HEADS * HD), D ** -0.5, 0.125, ((0, 8), (1, 4)))
    key_weight = bell_draw(splits[5], (D, KV_HEADS * HD), D ** -0.5, 0.125, ((0, 8), (1, 4)))
    value_weight = bell_draw(splits[6], (D, KV_HEADS * HD), D ** -0.5, 0.125, ((0, 8), (1, 4)))
    out_weight = bell_draw(splits[7], (HEADS * HD, D), (max(HEADS * HD * 16 // PAD, 1)) ** -0.5, 1.25, ((0, 4), (1, 8)))
    ffn_gain = jnp.clip(1.0 + 0.1 * jax.random.normal(splits[8], (D,), jnp.float32), 0.5, 1.5).astype(jnp.bfloat16)
    gate_weight = bell_draw(splits[9], (D, FF), D ** -0.5, 0.125, ((0, 8), (1, 4)))
    up_weight = bell_draw(splits[10], (D, FF), D ** -0.5, 0.125, ((0, 8), (1, 4)))
    down_weight = bell_draw(splits[11], (FF, D), FF ** -0.5, 0.078125, ((0, 4), (1, 8)))
    return {"tokens": tokens, "lengths": lengths, "cotangent": cotangent, "attn_gain": attn_gain, "query_weight": query_weight, "key_weight": key_weight, "value_weight": value_weight, "out_weight": out_weight, "ffn_gain": ffn_gain, "gate_weight": gate_weight, "up_weight": up_weight, "down_weight": down_weight}


EPSILON = 1e-05
THETA_BASE = 10000.0
NEGATIVE = -1e+30

@jax.custom_vjp
def low(v):
    return lax.optimization_barrier(v.astype(jnp.bfloat16)).astype(jnp.float32)

@jax.custom_vjp
def low_back(v):
    return v

def low_keep(v):
    return (low(v), None)

def low_pass(kept, grad):
    return (grad,)

def back_keep(v):
    return (v, None)

def back_low(kept, grad):
    return (low(grad),)
low.defvjp(low_keep, low_pass)
low_back.defvjp(back_keep, back_low)

def matmul_high(left, right):
    return jnp.dot(left, right, precision=lax.Precision.HIGHEST, preferred_element_type=jnp.float32)

def norm_rows(values, gain):
    return values * lax.rsqrt(lax.optimization_barrier(jnp.mean(values * values, axis=-1, keepdims=True)) + EPSILON) * gain

def rotate(values, cosine, sine):
    half = values.shape[-1] // 2
    first = values[..., :half]
    second = values[..., half:]
    return jnp.concatenate([first * cosine - second * sine, second * cosine + first * sine], axis=-1)

def attend(block):
    queries, key_rows, value_rows, length = block
    slots = jnp.arange(PAD)
    allowed = (slots[None, :] <= slots[:, None]) & (slots[:, None] - slots[None, :] < WINDOW) & (slots[None, :] < length)
    scores = jnp.einsum('gtd,pd->gtp', queries, key_rows, precision=lax.Precision.HIGHEST) * HD ** (-0.5)
    scores = low_back(scores)
    scores = jnp.where(allowed[None], scores, NEGATIVE)
    top_score = lax.optimization_barrier(jnp.max(scores, axis=-1, keepdims=True))
    exponent = jnp.exp(scores - top_score)
    probs = low(exponent / lax.optimization_barrier(jnp.sum(exponent, axis=-1, keepdims=True)))
    return jnp.einsum('gtp,pd->gtd', probs, value_rows, precision=lax.Precision.HIGHEST)

def forward(inputs, attn_gain, query_weight, key_weight, value_weight, out_weight, ffn_gain, gate_weight, up_weight, down_weight, seq_lengths):
    batch = inputs.shape[0]
    group_size = HEADS // KV_HEADS
    flat = inputs.reshape(batch * PAD, D)
    normed_one = low(norm_rows(flat, attn_gain))
    query_proj = low_back(matmul_high(normed_one, query_weight))
    key_proj = low_back(matmul_high(normed_one, key_weight))
    value_proj = low(low_back(matmul_high(normed_one, value_weight)))
    half = HD // 2
    freq = THETA_BASE ** (-jnp.arange(half, dtype=jnp.float32) * 2.0 / HD)
    angle = jnp.arange(PAD, dtype=jnp.float32)[:, None] * freq[None, :]
    cosine = jnp.cos(angle)[:, None, :]
    sine = jnp.sin(angle)[:, None, :]
    query_rot = low(rotate(query_proj.reshape(batch, PAD, HEADS, HD), cosine, sine))
    key_rot = low(rotate(key_proj.reshape(batch, PAD, KV_HEADS, HD), cosine, sine))
    value_rows = value_proj.reshape(batch, PAD, KV_HEADS, HD)
    query_blocks = query_rot.reshape(batch, PAD, KV_HEADS, group_size, HD).transpose(0, 2, 3, 1, 4).reshape(batch * KV_HEADS, group_size, PAD, HD)
    key_blocks = key_rot.transpose(0, 2, 1, 3).reshape(batch * KV_HEADS, PAD, HD)
    value_blocks = value_rows.transpose(0, 2, 1, 3).reshape(batch * KV_HEADS, PAD, HD)
    block_lengths = jnp.repeat(seq_lengths, KV_HEADS)
    attended = lax.map(jax.checkpoint(attend), (query_blocks, key_blocks, value_blocks, block_lengths))
    attended = attended.reshape(batch, KV_HEADS, group_size, PAD, HD).transpose(0, 3, 1, 2, 4).reshape(batch * PAD, HEADS * HD)
    attended = low_back(low(attended))
    hidden = flat + low_back(matmul_high(attended, out_weight))
    normed_two = low(norm_rows(hidden, ffn_gain))
    gate_proj = low_back(matmul_high(normed_two, gate_weight))
    up_proj = low_back(matmul_high(normed_two, up_weight))
    activation = low(jax.nn.silu(gate_proj) * up_proj)
    return (hidden + matmul_high(activation, down_weight)).reshape(batch, PAD, D)

def reference(tokens, lengths, cotangent, attn_gain, query_weight, key_weight, value_weight, out_weight, ffn_gain, gate_weight, up_weight, down_weight):
    batch = MICRO * SEQS
    inputs = tokens.astype(jnp.float32).reshape(batch, PAD, D)
    seq_lengths = lengths.reshape(batch).astype(jnp.int32)
    live_rows = (jnp.arange(PAD)[None, :] < seq_lengths[:, None]).astype(jnp.float32)

    def run(inputs, gain_one, w_query, w_key, w_value, w_out, gain_two, w_gate, w_up, w_down):
        return forward(inputs, gain_one, w_query, w_key, w_value, w_out, gain_two, w_gate, w_up, w_down, seq_lengths)
    output, pullback = jax.vjp(run, inputs, attn_gain.astype(jnp.float32), query_weight.astype(jnp.float32), key_weight.astype(jnp.float32), value_weight.astype(jnp.float32), out_weight.astype(jnp.float32), ffn_gain.astype(jnp.float32), gate_weight.astype(jnp.float32), up_weight.astype(jnp.float32), down_weight.astype(jnp.float32))
    grads = pullback(cotangent.astype(jnp.float32).reshape(batch, PAD, D) * live_rows[:, :, None])
    mixed = output.astype(jnp.bfloat16).reshape(MICRO, SEQS, PAD, D)
    token_grad = grads[0].reshape(MICRO, SEQS, PAD, D)
    return (mixed, token_grad, grads[1], grads[2], grads[3], grads[4], grads[5], grads[6], grads[7], grads[8], grads[9])
```

```python
import jax
import jax.numpy as jnp
from jax import lax
from jax.sharding import PartitionSpec as P

HD = 80
WINDOW = 4096

EPSILON = 1e-05
THETA_BASE = 10000.0
NEGATIVE = -1e30
LOW = jnp.bfloat16


def dot(left, right, a, b):
    return lax.dot_general(
        left, right, (((a,), (b,)), ((), ())), preferred_element_type=jnp.float32
    )


def tables(positions, width):
    half = width // 2
    freq = THETA_BASE ** (-jnp.arange(half, dtype=jnp.float32) * 2.0 / width)
    angle = positions.astype(jnp.float32)[:, None] * freq[None, :]
    return (jnp.cos(angle)[None, :, None, :], jnp.sin(angle)[None, :, None, :])


def rotate(values, cosine, sine):
    half = values.shape[-1] // 2
    first = values[..., :half]
    second = values[..., half:]
    return jnp.concatenate(
        [first * cosine - second * sine, second * cosine + first * sine], axis=-1
    )


def take_chunk(rows, index, size):
    return lax.dynamic_slice_in_dim(rows, index * size, size, axis=0)


def line_scatter(partial):
    n = lax.axis_size("head")
    z = lax.axis_index("head")
    size = partial.shape[0] // n
    up = down = None
    for step in range(n - 1):
        rising = take_chunk(partial, n - 1 - step + z, size)
        falling = take_chunk(partial, step + z - (n - 1), size)
        if step:
            rising = (rising.astype(jnp.float32) + up.astype(jnp.float32)).astype(LOW)
            falling = (falling.astype(jnp.float32) + down.astype(jnp.float32)).astype(LOW)
        up = lax.ppermute(rising, "head", [(i, i + 1) for i in range(step + 1)])
        down = lax.ppermute(
            falling, "head", [(i, i - 1) for i in range(n - 1 - step, n)]
        )
    mine = take_chunk(partial, z, size).astype(jnp.float32)
    return mine + up.astype(jnp.float32) + down.astype(jnp.float32)


def line_gather(chunk):
    n = lax.axis_size("head")
    z = lax.axis_index("head")
    size = chunk.shape[0]
    ups, downs = [], []
    up = down = chunk
    for step in range(n - 1):
        up = lax.ppermute(up, "head", [(i, i + 1) for i in range(step, n - 1)])
        down = lax.ppermute(down, "head", [(i, i - 1) for i in range(1, n - step)])
        ups.append(up)
        downs.append(down)
    whole = jnp.zeros((n * size,) + chunk.shape[1:], chunk.dtype)
    whole = lax.dynamic_update_slice_in_dim(whole, chunk, z * size, axis=0)
    for step in range(n - 1):
        got = jnp.where(z > step, ups[step], downs[n - 2 - step])
        place = lax.rem(z - 1 - step + n, n)
        whole = lax.dynamic_update_slice_in_dim(whole, got, place * size, axis=0)
    return whole


def norm_scale(values):
    return lax.rsqrt(jnp.mean(values * values, axis=-1, keepdims=True) + EPSILON)


def norm_back(grad, gain, normed, scale):
    scaled = grad * gain
    return scale * (scaled - normed * jnp.mean(scaled * normed, axis=-1, keepdims=True))


def per_device(
    tokens,
    lengths,
    cotangent,
    attn_gain,
    query_weight,
    key_weight,
    value_weight,
    out_weight,
    ffn_gain,
    gate_weight,
    up_weight,
    down_weight,
):
    micro_count, seq_count, local_tokens, width = tokens.shape
    z = lax.axis_index("head")
    lines = lax.axis_size("head")
    q_cols = query_weight.shape[1]
    kv_cols = key_weight.shape[1]
    units = gate_weight.shape[1]

    qkv_shard = jnp.concatenate([query_weight, key_weight, value_weight], axis=1)
    full_qkv = lax.all_gather(qkv_shard, "ctx", axis=0, tiled=True)
    gains = lax.all_gather(jnp.stack([attn_gain, ffn_gain]), "ctx", axis=1, tiled=True)
    gain_attn = gains[0].astype(jnp.float32)
    gain_ffn = gains[1].astype(jnp.float32)
    full_out = lax.all_gather(out_weight.T, "ctx", axis=0, tiled=True)
    full_gate = lax.all_gather(gate_weight, "ctx", axis=0, tiled=True)
    full_up = lax.all_gather(up_weight, "ctx", axis=0, tiled=True)
    full_down = lax.all_gather(down_weight.T, "ctx", axis=0, tiled=True)

    local_heads = q_cols // HD
    local_groups = kv_cols // HD
    group_size = local_heads // local_groups
    span_total = local_tokens * lax.axis_size("ctx")
    first_slot = lax.axis_index("ctx") * local_tokens
    query_slots = first_slot + jnp.arange(local_tokens)
    key_slots = jnp.arange(span_total)
    cosine, sine = tables(query_slots, HD)
    scale = HD ** (-0.5)
    piece_rows = seq_count * local_tokens
    rows = micro_count * piece_rows
    chunk = piece_rows // lines

    flat = tokens.reshape(rows, width)
    resid = flat.astype(jnp.float32)
    normed_one = resid * norm_scale(resid)
    input_one = (normed_one * gain_attn).astype(LOW)
    qkv = dot(input_one, full_qkv, 1, 0)
    batch = micro_count * seq_count
    query_rot = rotate(
        qkv[:, :q_cols].reshape(batch, local_tokens, local_heads, HD), cosine, sine
    ).astype(LOW)
    key_rot = rotate(
        qkv[:, q_cols : q_cols + kv_cols].reshape(batch, local_tokens, local_groups, HD),
        cosine,
        sine,
    ).astype(LOW)
    value_low = qkv[:, q_cols + kv_cols :].astype(LOW)
    kv = jnp.concatenate([key_rot.reshape(rows, kv_cols), value_low], axis=1)
    kv_all = lax.all_gather(
        kv.reshape(batch, local_tokens, 2 * kv_cols), "ctx", axis=1, tiled=True
    )

    live = (
        query_slots[None, None, :] < lengths[:, :, None]
    ).astype(jnp.float32).reshape(rows, 1)
    grad_out = (cotangent.reshape(rows, width).astype(jnp.float32) * live).astype(LOW)

    pieces = range(micro_count)
    saved = []
    hidden_parts = []
    for piece in pieces:
        seqs = slice(piece * seq_count, (piece + 1) * seq_count)
        query = query_rot[seqs].reshape(
            seq_count, local_tokens, local_groups, group_size, HD
        )
        key_all = kv_all[seqs, :, :kv_cols].reshape(seq_count, span_total, local_groups, HD)
        value_all = kv_all[seqs, :, kv_cols:].reshape(seq_count, span_total, local_groups, HD)
        allowed = (
            (key_slots[None, None, :] <= query_slots[None, :, None])
            & (query_slots[None, :, None] - key_slots[None, None, :] < WINDOW)
            & (key_slots[None, None, :] < lengths[piece][:, None, None])
        )[:, None, None]
        scores = (
            jnp.einsum("stkgd,spkd->skgtp", query, key_all, preferred_element_type=jnp.float32)
            * scale
        )
        scores = jnp.where(allowed, scores, NEGATIVE)
        top_score = jnp.max(scores, axis=-1, keepdims=True)
        exponent = jnp.exp(scores - top_score)
        total_weight = jnp.sum(exponent, axis=-1, keepdims=True)
        probs_low = (exponent / total_weight).astype(LOW)
        log_total = top_score + jnp.log(total_weight)
        attended = jnp.einsum(
            "skgtp,spkd->stkgd", probs_low, value_all, preferred_element_type=jnp.float32
        )
        attended_low = attended.reshape(piece_rows, q_cols).astype(LOW)
        saved.append((query, key_all, value_all, allowed, log_total, attended_low))
        branch = dot(attended_low, full_out, 1, 1).astype(LOW)
        summed = line_scatter(branch)
        piece_tokens = take_chunk(flat[piece * piece_rows : (piece + 1) * piece_rows], z, chunk)
        hidden_parts.append(piece_tokens.astype(jnp.float32) + summed)

    inputs_two, mixed_parts, grads_two = [], [], []
    acts, grad_gates, grad_ups = [], [], []
    grad_hidden_parts, gain_two_terms, grads_low = [], [], []
    for piece in pieces:
        hidden = hidden_parts[piece]
        scale_two = norm_scale(hidden)
        normed_two = hidden * scale_two
        input_two = line_gather((normed_two * gain_ffn).astype(LOW))
        inputs_two.append(input_two)
        dy = grad_out[piece * piece_rows : (piece + 1) * piece_rows]
        gate = dot(input_two, full_gate, 1, 0)
        up = dot(input_two, full_up, 1, 0)
        sigmoid = jax.nn.sigmoid(gate)
        silu = gate * sigmoid
        act = (silu * up).astype(LOW)
        grad_act = dot(dy, full_down, 1, 0)
        grad_gate = (grad_act * up * sigmoid * (1.0 + gate * (1.0 - sigmoid))).astype(LOW)
        grad_up = (grad_act * silu).astype(LOW)
        acts.append(act)
        grad_gates.append(grad_gate)
        grad_ups.append(grad_up)
        grad_two = line_scatter(
            (dot(grad_gate, full_gate, 1, 1) + dot(grad_up, full_up, 1, 1)).astype(LOW)
        )
        ffn = line_scatter(dot(act, full_down, 1, 1).astype(LOW))
        mixed_parts.append(line_gather((hidden + ffn).astype(LOW)))
        gain_two_terms.append(jnp.sum(grad_two * normed_two, axis=0))
        grad_hidden = take_chunk(dy, z, chunk).astype(jnp.float32) + norm_back(
            grad_two, gain_ffn, normed_two, scale_two
        )
        grad_hidden_parts.append(grad_hidden)
        grads_low.append(line_gather(grad_hidden.astype(LOW)))

    act_all = jnp.concatenate(acts, axis=0)
    gate_back = jnp.concatenate(grad_gates, axis=0)
    up_back = jnp.concatenate(grad_ups, axis=0)
    two_all = jnp.concatenate(inputs_two, axis=0)
    hidden_low = jnp.concatenate(grads_low, axis=0)
    attended_all = jnp.concatenate([s[5] for s in saved], axis=0)

    def scatter_weight(term):
        return lax.psum_scatter(term, "ctx", scatter_dimension=0, tiled=True)

    down_grad = scatter_weight(dot(grad_out, act_all, 0, 0).astype(LOW))
    gate_grad = scatter_weight(dot(two_all, gate_back, 0, 0).astype(LOW))
    up_grad = scatter_weight(dot(two_all, up_back, 0, 0).astype(LOW))
    out_grad = scatter_weight(dot(hidden_low, attended_all, 0, 0).astype(LOW))

    query_parts, kv_parts = [], []
    for piece in pieces:
        query, key_all, value_all, allowed, log_total, attended_low = saved[piece]
        grad_att = dot(grads_low[piece], full_out, 1, 0).astype(LOW)
        grad_att = grad_att.reshape(seq_count, local_tokens, local_groups, group_size, HD)
        scores = (
            jnp.einsum("stkgd,spkd->skgtp", query, key_all, preferred_element_type=jnp.float32)
            * scale
        )
        scores = jnp.where(allowed, scores, NEGATIVE)
        probs = jnp.exp(scores - log_total)
        grad_probs = jnp.einsum(
            "stkgd,spkd->skgtp", grad_att, value_all, preferred_element_type=jnp.float32
        )
        row_dot = jnp.sum(probs * grad_probs, axis=-1, keepdims=True)
        grad_scores = (probs * (grad_probs - row_dot)).astype(LOW)
        grad_query = (
            jnp.einsum("skgtp,spkd->stkgd", grad_scores, key_all, preferred_element_type=jnp.float32)
            * scale
        )
        key_partial = (
            jnp.einsum("skgtp,stkgd->spkd", grad_scores, query, preferred_element_type=jnp.float32)
            * scale
        )
        value_partial = jnp.einsum(
            "skgtp,stkgd->spkd", probs.astype(LOW), grad_att, preferred_element_type=jnp.float32
        )
        query_parts.append(
            rotate(
                grad_query.reshape(seq_count, local_tokens, local_heads, HD), cosine, -sine
            ).reshape(piece_rows, q_cols).astype(LOW)
        )
        both = jnp.concatenate(
            [
                key_partial.reshape(seq_count, span_total, kv_cols),
                value_partial.reshape(seq_count, span_total, kv_cols),
            ],
            axis=-1,
        ).astype(LOW)
        kv_parts.append(both)
    kv_back = lax.psum_scatter(
        jnp.concatenate(kv_parts, axis=0), "ctx", scatter_dimension=1, tiled=True
    )
    key_back = rotate(
        kv_back[..., :kv_cols].astype(jnp.float32).reshape(batch, local_tokens, local_groups, HD),
        cosine,
        -sine,
    ).reshape(rows, kv_cols).astype(LOW)
    value_back = kv_back[..., kv_cols:].reshape(rows, kv_cols)
    qkv_back = jnp.concatenate(
        [jnp.concatenate(query_parts, axis=0), key_back, value_back], axis=1
    )
    qkv_grad = scatter_weight(dot(input_one, qkv_back, 0, 0).astype(LOW)).astype(jnp.float32)

    token_parts = []
    gain_one_terms = []
    for piece in pieces:
        span = slice(piece * piece_rows, (piece + 1) * piece_rows)
        grad_one = line_scatter(dot(qkv_back[span], full_qkv, 1, 1).astype(LOW))
        piece_tokens = take_chunk(flat[span], z, chunk).astype(jnp.float32)
        scale_one = norm_scale(piece_tokens)
        normed = piece_tokens * scale_one
        gain_one_terms.append(jnp.sum(grad_one * normed, axis=0))
        back = grad_hidden_parts[piece] + norm_back(grad_one, gain_attn, normed, scale_one)
        token_parts.append(line_gather(back.astype(LOW)))
    gain_terms = lax.psum(
        jnp.stack([sum(gain_one_terms), sum(gain_two_terms)]), ("head", "ctx")
    )
    gain_terms = lax.dynamic_slice_in_dim(
        gain_terms, lax.axis_index("ctx") * attn_gain.shape[0], attn_gain.shape[0], axis=1
    )
    mixed = jnp.stack(mixed_parts, axis=0).reshape(tokens.shape)
    token_grad = jnp.stack(token_parts, axis=0).reshape(tokens.shape).astype(jnp.float32)
    return (
        mixed,
        token_grad,
        gain_terms[0],
        qkv_grad[:, :q_cols],
        qkv_grad[:, q_cols : q_cols + kv_cols],
        qkv_grad[:, q_cols + kv_cols :],
        out_grad.T.astype(jnp.float32),
        gain_terms[1],
        gate_grad.astype(jnp.float32),
        up_grad.astype(jnp.float32),
        down_grad.T.astype(jnp.float32),
    )


def solution(mesh):
    placed = (
        P(None, None, "ctx", None),
        P(),
        P(None, None, "ctx", None),
        P("ctx"),
        P("ctx", "head"),
        P("ctx", "head"),
        P("ctx", "head"),
        P("head", "ctx"),
        P("ctx"),
        P("ctx", "head"),
        P("ctx", "head"),
        P("head", "ctx"),
    )
    return jax.shard_map(
        per_device,
        mesh=mesh,
        in_specs=placed,
        out_specs=(
            P(None, None, "ctx", None),
            P(None, None, "ctx", None),
            P("ctx"),
            P("ctx", "head"),
            P("ctx", "head"),
            P("ctx", "head"),
            P("head", "ctx"),
            P("ctx"),
            P("ctx", "head"),
            P("ctx", "head"),
            P("head", "ctx"),
        ),
        check_vma=False,
    )
```

```python
import functools

import jax
import jax.numpy as jnp
from jax import lax
from jax.experimental.layout import Layout, with_layout_constraint
from jax.experimental import pallas as pl
from jax.experimental.pallas import tpu as pltpu
from jax.sharding import PartitionSpec as P

HD = 80
WINDOW = 4096

EPSILON = 1e-05
THETA_BASE = 10000.0
NEGATIVE = -1e30
LOG2E = 1.4426950408889634
LOW = jnp.bfloat16
VMEM_LIMIT = 48 * 1024 * 1024
COST = 2


def dot(left, right, a, b):
    return lax.dot_general(
        left, right, (((a,), (b,)), ((), ())), preferred_element_type=jnp.float32
    )


def after(value, *others):
    if not others:
        return value
    return lax.optimization_barrier((value, others))[0]


def angles(positions):
    half = HD // 2
    freq = THETA_BASE ** (-jnp.arange(half, dtype=jnp.float32) * 2.0 / HD)
    angle = positions.astype(jnp.float32)[:, None] * freq[None, :]
    return jnp.cos(angle), jnp.sin(angle)


def add_low(*terms):
    return sum(term.astype(jnp.float32) for term in terms).astype(LOW)


def flip(bit):
    n = lax.axis_size("ctx")
    return [(i, i ^ bit) for i in range(n)]


def chip_bits():
    bits, bit = [], 2
    while bit < lax.axis_size("ctx"):
        bits.append(bit)
        bit *= 2
    return bits


def cube_gather(part, bits):
    own, places = part[None], [0]
    for bit in bits:
        got = lax.ppermute(own, "ctx", flip(bit))
        own = jnp.concatenate([own, got], axis=0)
        places = places + [place ^ (bit // 2) for place in places]
    order = [places.index(m) for m in range(len(places))]
    if order != sorted(order):
        own = jnp.stack([own[at] for at in order], axis=0)
    return own, lax.ppermute(own, "ctx", flip(1))


def line_bits():
    bits, bit = [], 1
    while bit < lax.axis_size("head"):
        bits.append(bit)
        bit *= 2
    return bits


def line_swap(value, bit):
    n = lax.axis_size("head")
    return lax.ppermute(value, "head", [(i, i ^ bit) for i in range(n)])


def line_place(z):
    place = z * 0
    for bit in line_bits():
        place = place * 2 + lax.rem(z // bit, 2)
    return place


class Scatter:
    def __init__(self, partial, *others):
        self.held = after(partial, *others)
        self.bits = line_bits()
        self.send()

    def send(self):
        half = self.held.shape[0] // 2
        mine = lax.rem(lax.axis_index("head") // self.bits[0], 2)
        self.landed = line_swap(
            take_chunk(self.held, 1 - mine, half).astype(LOW), self.bits[0]
        )
        self.kept = take_chunk(self.held, mine, half).astype(jnp.float32)
        self.bits = self.bits[1:]

    def land(self):
        self.held = self.kept + self.landed.astype(jnp.float32)

    def next(self, *others):
        self.landed = after(self.landed, *others)
        self.land()
        self.send()
        return self

    def finish(self, *others):
        while self.bits:
            self.next()
        self.landed = after(self.landed, *others)
        self.land()
        return self.held


class Gather:
    def __init__(self, chunk, *others):
        self.held = after(chunk, *others)
        self.bits = line_bits()[::-1]
        self.send()

    def send(self):
        self.mine = lax.rem(lax.axis_index("head") // self.bits[0], 2)
        self.landed = line_swap(self.held, self.bits[0])
        self.bits = self.bits[1:]

    def land(self):
        first = jnp.where(self.mine == 0, self.held, self.landed)
        second = jnp.where(self.mine == 0, self.landed, self.held)
        self.held = jnp.concatenate([first, second], axis=0)

    def next(self, *others):
        self.landed = after(self.landed, *others)
        self.land()
        self.send()
        return self

    def finish(self, *others):
        while self.bits:
            self.next()
        self.landed = after(self.landed, *others)
        self.land()
        return self.held


class ChainScatter:
    def __init__(self, partial, *others):
        self.partial = after(partial, *others)
        self.step = 0
        self.send()

    def block(self, z):
        n = lax.axis_size("head")
        size = self.partial.shape[0] // n
        return take_chunk(self.partial, line_place(jnp.clip(z, 0, n - 1)), size)

    def send(self):
        n = lax.axis_size("head")
        z = lax.axis_index("head")
        step = self.step
        rising = self.block(n - 1 - step + z)
        falling = self.block(step + z - (n - 1))
        if step:
            rising = add_low(rising, self.landed[0])
            falling = add_low(falling, self.landed[1])
        self.landed = (
            lax.ppermute(rising, "head", [(i, i + 1) for i in range(step + 1)]),
            lax.ppermute(falling, "head", [(i, i - 1) for i in range(n - 1 - step, n)]),
        )
        self.step += 1

    def next(self, *others):
        self.landed = (after(self.landed[0], *others), self.landed[1])
        self.send()
        return self

    def finish(self, *others):
        while self.step < lax.axis_size("head") - 1:
            self.next()
        mine = after(self.block(lax.axis_index("head")), *others)
        return sum(part.astype(jnp.float32) for part in (mine,) + self.landed)


class ChainGather:
    def __init__(self, chunk, *others):
        self.chunk = after(chunk, *others)
        self.landed = (self.chunk, self.chunk)
        self.got = []
        self.send()

    def send(self):
        n = lax.axis_size("head")
        step = len(self.got)
        self.landed = (
            lax.ppermute(self.landed[0], "head", [(i, i + 1) for i in range(step, n - 1)]),
            lax.ppermute(self.landed[1], "head", [(i, i - 1) for i in range(1, n - step)]),
        )
        self.got.append(self.landed)

    def next(self, *others):
        self.landed = (after(self.landed[0], *others), self.landed[1])
        self.send()
        return self

    def finish(self, *others):
        n = lax.axis_size("head")
        z = lax.axis_index("head")
        while len(self.got) < n - 1:
            self.next()
        size = self.chunk.shape[0]
        whole = jnp.zeros((n * size,) + self.chunk.shape[1:], self.chunk.dtype)
        whole = lax.dynamic_update_slice_in_dim(
            whole, after(self.chunk, *others), line_place(z) * size, axis=0
        )
        for step in range(n - 1):
            block = jnp.where(z > step, self.got[step][0], self.got[n - 2 - step][1])
            at = line_place(lax.rem(z - 1 - step + n, n)) * size
            whole = lax.dynamic_update_slice_in_dim(whole, block, at, axis=0)
        return whole


class Reduce:
    def __init__(self, own, other, bits):
        self.bits = bits[::-1]
        self.kept = own
        self.landed = lax.ppermute(other, "ctx", flip(1))

    def next(self, *others):
        landed = after(self.landed, *others)
        bit, self.bits = self.bits[0], self.bits[1:]
        half = self.kept.shape[0] // 2
        sent = add_low(self.kept[half:], landed[half:])
        self.kept = add_low(self.kept[:half], landed[:half])
        self.landed = lax.ppermute(sent, "ctx", flip(bit))

    def finish(self):
        while self.bits:
            self.next()
        return self.kept[0], self.landed[0]


def project_kernel(tokens_ref, gain_ref, weight_ref, cos_ref, ahead_ref, behind_ref, normed_ref, query_ref, kv_ref):
    values = tokens_ref[...].astype(jnp.float32)
    scale = lax.rsqrt(jnp.mean(values * values, axis=-1, keepdims=True) + EPSILON)
    normed = (values * scale * gain_ref[...]).astype(LOW)
    normed_ref[...] = normed
    out = dot(normed, weight_ref[...], 1, 0)
    local, padded = cos_ref.shape
    q_cols, kv_cols = query_ref.shape[1], kv_ref.shape[1]
    for start in range(0, out.shape[0], local):
        part = out[start : start + local]
        turned = (
            part * cos_ref[...]
            + pltpu.roll(part, padded - HD // 2, 1) * ahead_ref[...]
            + pltpu.roll(part, HD // 2, 1) * behind_ref[...]
        ).astype(LOW)
        query_ref[start : start + local, :] = turned[:, :q_cols]
        kv_ref[start : start + local, :] = turned[:, q_cols : q_cols + kv_cols]


def project(flat, gain, weight, cos, ahead, behind, pieces, q_cols, kv_cols):
    rows, width = flat.shape
    size = rows // pieces
    padded = weight.shape[1]
    whole = lambda shape: pl.BlockSpec(shape, lambda i: (0,) * len(shape))
    strip = lambda columns: pl.BlockSpec((size, columns), lambda i: (i, 0))
    return pl.pallas_call(
        project_kernel,
        grid=(pieces,),
        in_specs=[
            strip(width),
            whole((1, width)),
            whole((width, padded)),
            whole(cos.shape),
            whole(cos.shape),
            whole(cos.shape),
        ],
        out_specs=[strip(width), strip(q_cols), strip(kv_cols)],
        out_shape=[
            jax.ShapeDtypeStruct((rows, width), LOW),
            jax.ShapeDtypeStruct((rows, q_cols), LOW),
            jax.ShapeDtypeStruct((rows, kv_cols), LOW),
        ],
        compiler_params=pltpu.CompilerParams(vmem_limit_bytes=VMEM_LIMIT),
        cost_estimate=pl.CostEstimate(
            flops=2 * rows * width * padded,
            bytes_accessed=4 * rows * width + 2 * width * padded,
            transcendentals=0,
        ),
        name="project",
    )(flat, gain, weight, cos, ahead, behind)


def feed_kernel(input_ref, grad_ref, gate_ref, up_ref, down_ref, act_ref, grad_gate_ref, grad_up_ref):
    gate = dot(input_ref[...], gate_ref[...], 1, 0)
    up = dot(input_ref[...], up_ref[...], 1, 0)
    grad_act = dot(grad_ref[...], down_ref[...], 1, 0)
    sigmoid = jax.nn.sigmoid(gate)
    silu = gate * sigmoid
    act_ref[...] = (silu * up).astype(LOW)
    grad_gate_ref[...] = (grad_act * up * sigmoid * (1.0 + gate * (1.0 - sigmoid))).astype(LOW)
    grad_up_ref[...] = (grad_act * silu).astype(LOW)


def feed(inputs, grads, gate, up, down):
    rows, width = inputs.shape
    units = gate.shape[1]
    tile = 256
    whole = pl.BlockSpec((rows, width), lambda i: (0, 0))
    weight = pl.BlockSpec((width, tile), lambda i: (0, i))
    out = pl.BlockSpec((rows, tile), lambda i: (0, i))
    return pl.pallas_call(
        feed_kernel,
        grid=((units + tile - 1) // tile,),
        in_specs=[whole, whole, weight, weight, weight],
        out_specs=[out, out, out],
        out_shape=[jax.ShapeDtypeStruct((rows, units), LOW)] * 3,
        compiler_params=pltpu.CompilerParams(vmem_limit_bytes=VMEM_LIMIT),
        cost_estimate=pl.CostEstimate(
            flops=6 * rows * width * units // COST,
            bytes_accessed=(6 * width * units + 4 * rows * width + 6 * rows * units) // COST,
            transcendentals=0,
        ),
        name="feed",
    )(inputs, grads, gate, up, down)


def back_kernel(*refs):
    out_ref = refs[-1]
    count = (len(refs) - 1) // 2
    total = dot(refs[0][...], refs[count][...], 1, 1)
    for at in range(1, count):
        total += dot(refs[at][...], refs[count + at][...], 1, 1)
    out_ref[...] = total.astype(LOW)


def back_through(values, weights):
    rows, units = values[0].shape
    width = weights[0].shape[0]
    tile = 256
    count = len(values)
    return pl.pallas_call(
        back_kernel,
        grid=((width + tile - 1) // tile,),
        in_specs=[pl.BlockSpec((rows, units), lambda i: (0, 0))] * count
        + [pl.BlockSpec((tile, units), lambda i: (i, 0))] * count,
        out_specs=pl.BlockSpec((rows, tile), lambda i: (0, i)),
        out_shape=jax.ShapeDtypeStruct((rows, width), LOW),
        compiler_params=pltpu.CompilerParams(vmem_limit_bytes=VMEM_LIMIT),
        cost_estimate=pl.CostEstimate(
            flops=2 * count * rows * width * units // COST,
            bytes_accessed=(2 * count * (width + rows) * units + 2 * rows * width) // COST,
            transcendentals=0,
        ),
        name="back_through",
    )(*values, *weights)


def join_kernel(query_ref, kept_ref, landed_ref, cos_ref, ahead_ref, behind_ref, out_ref):
    q_cols, kv_cols = query_ref.shape[1], kept_ref.shape[1]
    local, padded = cos_ref.shape
    out_ref[:, :q_cols] = query_ref[...]
    for start in range(0, kept_ref.shape[0], local):
        rows = slice(start, start + local)
        part = kept_ref[rows, :].astype(jnp.float32) + landed_ref[rows, :].astype(jnp.float32)
        if padded > kv_cols:
            part = jnp.concatenate(
                [part, jnp.zeros((local, padded - kv_cols), jnp.float32)], axis=1
            )
        turned = (
            part * cos_ref[...]
            - pltpu.roll(part, padded - HD // 2, 1) * ahead_ref[...]
            - pltpu.roll(part, HD // 2, 1) * behind_ref[...]
        ).astype(LOW)
        out_ref[rows, q_cols : q_cols + kv_cols] = turned[:, :kv_cols]


def join_back(query, kept, landed, cos, ahead, behind):
    rows, q_cols = query.shape
    return pl.pallas_call(
        join_kernel,
        out_shape=jax.ShapeDtypeStruct((rows, q_cols + kept.shape[1]), LOW),
        compiler_params=pltpu.CompilerParams(vmem_limit_bytes=VMEM_LIMIT),
        cost_estimate=pl.CostEstimate(flops=0, bytes_accessed=8 * kept.size, transcendentals=0),
        name="join_back",
    )(query, kept, landed, cos, ahead, behind)


def stack_heads(block, group, per):
    return jnp.concatenate(
        [block[:, (group * per + h) * HD : (group * per + h + 1) * HD] for h in range(per)],
        axis=0,
    )


def key_block(own_ref, other_ref, at, column):
    return jnp.concatenate(
        [own_ref[at, :, column : column + HD], other_ref[at, :, column : column + HD]],
        axis=0,
    )


def key_limits(meta_ref, slots_ref, local):
    me, length = meta_ref[0], meta_ref[1 + pl.program_id(0)]
    pair = 2 * local
    full = lax.div(jnp.minimum(me * local + 1, length), pair)
    some = lax.div(jnp.minimum((me + 1) * local, length) + pair - 1, pair)
    limit = jnp.minimum(slots_ref[...], length - 1)
    row = lax.broadcasted_iota(jnp.int32, (pair, 1), 0)
    core = lax.rem(me, 2)
    within = jnp.where(row < local, core * local + row, (1 - core) * local + row - local)
    return me, length, full, some, limit, within


def keep_allowed(scores, base, within, limit, slots, window):
    place = base + within
    allowed = place <= limit
    if window:
        allowed = allowed & (slots - place < WINDOW)
    return jnp.where(allowed, scores, NEGATIVE)


def attend_kernel(meta_ref, slots_ref, query_ref, own_ref, other_ref, att_ref, lse_ref, stacked, total, *, groups, per, window):
    local = query_ref.shape[0]
    pair = 2 * local
    kv_cols = groups * HD
    me, _, full, some, limit, within = key_limits(meta_ref, slots_ref, local)
    if window:
        full = full * 0
    factor = HD ** (-0.5) * LOG2E
    for g in range(groups):
        stacked[g] = stack_heads(query_ref[...], g, per)
        total[g] = jnp.zeros(total.shape[1:], jnp.float32)

    def step(m, carry, masked):
        at = jnp.bitwise_xor(m, lax.div(me, 2))
        out = []
        for g in range(groups):
            top, weight = carry[g]
            keys = key_block(own_ref, other_ref, at, g * HD)
            values = key_block(own_ref, other_ref, at, kv_cols + g * HD)
            scores = dot(keys, stacked[g], 1, 1) * factor
            if masked:
                scores = keep_allowed(scores, m * pair, within, limit, slots_ref[...], window)
            higher = jnp.maximum(top, jnp.max(scores, axis=0, keepdims=True))
            probs = jnp.exp2(scores - higher)
            shrink = jnp.exp2(top - higher)
            total[g] = total[g] * shrink + dot(values, probs.astype(LOW), 0, 0)
            out.append(
                (higher, weight * shrink + jnp.sum(probs, axis=0, keepdims=True))
            )
        return tuple(out)

    row = (1, per * local)
    carry = tuple(
        (jnp.full(row, NEGATIVE, jnp.float32), jnp.zeros(row, jnp.float32))
        for _ in range(groups)
    )
    carry = lax.fori_loop(0, full, lambda m, c: step(m, c, False), carry)
    carry = lax.fori_loop(full, some, lambda m, c: step(m, c, True), carry)
    for g in range(groups):
        top, weight = carry[g]
        lse_ref[0, g : g + 1, :] = top + jnp.log2(weight)
        out = (total[g] / weight).T.astype(LOW)
        for h in range(per):
            at = (g * per + h) * HD
            att_ref[:, at : at + HD] = out[h * local : (h + 1) * local]


def attend_back_kernel(
    meta_ref, slots_ref, cos_ref, sin_ref, query_ref, own_ref, other_ref, att_ref, grad_ref, lse_ref,
    grad_query_ref, grad_own_ref, grad_other_ref, stacked, stacked_grad, total, row_dot, *, groups, per, window,
):
    local = query_ref.shape[0]
    pair = 2 * local
    kv_cols = groups * HD
    me, length, full, some, limit, within = key_limits(meta_ref, slots_ref, local)
    if window:
        full = full * 0
    scale = HD ** (-0.5)
    live = me * local < length
    full = jnp.where(live, full, 0)
    some = jnp.where(live, some, 0)
    chips = own_ref.shape[0]
    chip = lax.div(me, 2)

    for g in range(groups):
        stacked[g] = stack_heads(query_ref[...], g, per)
        grads = stack_heads(grad_ref[...], g, per)
        stacked_grad[g] = grads
        product = grads.astype(jnp.float32) * stack_heads(att_ref[...], g, per).astype(jnp.float32)
        row_dot[g : g + 1, :] = jnp.sum(product.T, axis=0, keepdims=True)
        total[g] = jnp.zeros(total.shape[1:], jnp.float32)

    def clear(m, carry):
        at = jnp.bitwise_xor(m, chip)
        grad_own_ref[at] = jnp.zeros(grad_own_ref.shape[1:], LOW)
        grad_other_ref[at] = jnp.zeros(grad_other_ref.shape[1:], LOW)
        return carry

    def step(m, carry, masked):
        at = jnp.bitwise_xor(m, chip)
        for g in range(groups):
            keys = key_block(own_ref, other_ref, at, g * HD)
            values = key_block(own_ref, other_ref, at, kv_cols + g * HD)
            scores = dot(keys, stacked[g], 1, 1) * (scale * LOG2E)
            if masked:
                scores = keep_allowed(scores, m * pair, within, limit, slots_ref[...], window)
            probs = jnp.exp2(scores - lse_ref[0, g : g + 1, :])
            grad_probs = dot(values, stacked_grad[g], 1, 1)
            grad_scores = (probs * (grad_probs - row_dot[g : g + 1, :])).astype(LOW)
            grad_values = dot(probs.astype(LOW), stacked_grad[g], 1, 0).astype(LOW)
            grad_keys = (dot(grad_scores, stacked[g], 1, 0) * scale).astype(LOW)
            total[g] += dot(keys, grad_scores, 0, 0)
            for column, grads in ((g * HD, grad_keys), (kv_cols + g * HD, grad_values)):
                grad_own_ref[at, :, column : column + HD] = grads[:local]
                grad_other_ref[at, :, column : column + HD] = grads[local:]
        return carry

    lax.fori_loop(0, full, lambda m, c: step(m, c, False), 0)
    lax.fori_loop(full, some, lambda m, c: step(m, c, True), 0)
    lax.fori_loop(some, chips, clear, 0)
    half = HD // 2
    cos, sin = cos_ref[...], sin_ref[...]
    for g in range(groups):
        grads = total[g] * scale
        first, second = grads[:half], grads[half:]
        turned = jnp.concatenate(
            [first * cos + second * sin, second * cos - first * sin], axis=0
        ).T.astype(LOW)
        for h in range(per):
            at = (g * per + h) * HD
            grad_query_ref[:, at : at + HD] = turned[h * local : (h + 1) * local]


def attention_specs(seqs, local, q_cols, kv_both, chips, groups, columns):
    meta = pl.BlockSpec(memory_space=pltpu.SMEM)
    whole = lambda shape: pl.BlockSpec(shape, lambda s: (0,) * len(shape))
    queries = pl.BlockSpec((local, q_cols), lambda s: (s, 0))
    keys = pl.BlockSpec((chips, local, kv_both), lambda s: (0, s, 0))
    lse = pl.BlockSpec((1, groups, columns), lambda s: (s, 0, 0))
    return meta, whole, queries, keys, lse


def attend(meta, slots, query, own, other, groups, window):
    seqs = meta.shape[0] - 1
    rows, q_cols = query.shape
    local = rows // seqs
    chips, _, kv_both = own.shape
    per = q_cols // HD // groups
    columns = per * local
    smem, whole, queries, keys, lse = attention_specs(
        seqs, local, q_cols, kv_both, chips, groups, columns
    )
    pairs = rows * q_cols // HD * 2 * chips * local
    return pl.pallas_call(
        functools.partial(attend_kernel, groups=groups, per=per, window=window),
        grid=(seqs,),
        in_specs=[smem, whole((1, columns)), queries, keys, keys],
        out_specs=[queries, lse],
        out_shape=[
            jax.ShapeDtypeStruct((rows, q_cols), LOW),
            jax.ShapeDtypeStruct((seqs, groups, columns), jnp.float32),
        ],
        scratch_shapes=[
            pltpu.VMEM((groups, columns, HD), LOW),
            pltpu.VMEM((groups, HD, columns), jnp.float32),
        ],
        compiler_params=pltpu.CompilerParams(vmem_limit_bytes=VMEM_LIMIT),
        cost_estimate=pl.CostEstimate(
            flops=12 * pairs * HD, bytes_accessed=4 * own.size, transcendentals=pairs
        ),
        name="attend",
    )(meta, slots, query, own, other)


def attend_back(meta, slots, cos, sin, query, own, other, att, grad, lse_rows, groups, window):
    seqs = meta.shape[0] - 1
    rows, q_cols = query.shape
    local = rows // seqs
    chips, _, kv_both = own.shape
    per = q_cols // HD // groups
    columns = per * local
    smem, whole, queries, keys, lse = attention_specs(
        seqs, local, q_cols, kv_both, chips, groups, columns
    )
    pairs = rows * q_cols // HD * 2 * chips * local
    return pl.pallas_call(
        functools.partial(attend_back_kernel, groups=groups, per=per, window=window),
        grid=(seqs,),
        in_specs=[
            smem, whole((1, columns)), whole(cos.shape), whole(cos.shape),
            queries, keys, keys, queries, queries, lse,
        ],
        out_specs=[queries, keys, keys],
        out_shape=[
            jax.ShapeDtypeStruct((rows, q_cols), LOW),
            jax.ShapeDtypeStruct(own.shape, LOW),
            jax.ShapeDtypeStruct(own.shape, LOW),
        ],
        scratch_shapes=[
            pltpu.VMEM((groups, columns, HD), LOW),
            pltpu.VMEM((groups, columns, HD), LOW),
            pltpu.VMEM((groups, HD, columns), jnp.float32),
            pltpu.VMEM((groups, columns), jnp.float32),
        ],
        compiler_params=pltpu.CompilerParams(vmem_limit_bytes=VMEM_LIMIT),
        cost_estimate=pl.CostEstimate(
            flops=30 * pairs * HD, bytes_accessed=8 * own.size, transcendentals=pairs
        ),
        name="attend_back",
    )(meta, slots, cos, sin, query, own, other, att, grad, lse_rows)


def take_chunk(rows, index, size):
    return lax.dynamic_slice_in_dim(rows, index * size, size, axis=0)


def norm_scale(values):
    return lax.rsqrt(jnp.mean(values * values, axis=-1, keepdims=True) + EPSILON)


def norm_back(grad, gain, normed, scale):
    scaled = grad * gain
    return scale * (scaled - normed * jnp.mean(scaled * normed, axis=-1, keepdims=True))


def per_device(
    tokens,
    lengths,
    cotangent,
    attn_gain,
    query_weight,
    key_weight,
    value_weight,
    out_weight,
    ffn_gain,
    gate_weight,
    up_weight,
    down_weight,
):
    micro_count, seq_count, local_tokens, width = tokens.shape
    place = line_place(lax.axis_index("head"))
    me = lax.axis_index("ctx")
    lines = lax.axis_size("head")
    q_cols = query_weight.shape[1]
    kv_cols = key_weight.shape[1]
    used = q_cols + 2 * kv_cols
    padded = (used + 2 + 127) // 128 * 128

    qkv_shard = jnp.concatenate(
        [
            query_weight,
            key_weight,
            value_weight,
            attn_gain[:, None],
            ffn_gain[:, None],
            jnp.zeros((query_weight.shape[0], padded - used - 2), LOW),
        ],
        axis=1,
    )
    full_qkv = lax.all_gather(qkv_shard, "ctx", axis=0, tiled=True)
    full_out = lax.all_gather(out_weight.T, "ctx", axis=0, tiled=True)
    full_gate = lax.all_gather(gate_weight, "ctx", axis=0, tiled=True)
    full_up = lax.all_gather(up_weight, "ctx", axis=0, tiled=True)
    full_down = lax.all_gather(down_weight.T, "ctx", axis=0, tiled=True)
    gains = full_qkv[:, used : used + 2].T.astype(jnp.float32)
    gain_attn = gains[0:1]
    gain_ffn = gains[1:2]

    heads = q_cols // HD
    groups = kv_cols // HD
    per = heads // groups
    span_total = local_tokens * lax.axis_size("ctx")
    window = span_total > WINDOW
    query_slots = me * local_tokens + jnp.arange(local_tokens, dtype=jnp.int32)
    cosine, sine = angles(query_slots)
    piece_rows = seq_count * local_tokens
    rows = micro_count * piece_rows
    chunk = piece_rows // lines
    pieces = range(micro_count)

    nothing = jnp.zeros_like(sine)
    turning = heads + groups
    rest = padded - turning * HD
    cos_wide = jnp.concatenate(
        [cosine] * (2 * turning) + [jnp.ones((local_tokens, rest), jnp.float32)], axis=1
    )
    ahead = jnp.concatenate(
        [-sine, nothing] * turning + [jnp.zeros((local_tokens, rest), jnp.float32)], axis=1
    )
    behind = jnp.concatenate(
        [nothing, sine] * turning + [jnp.zeros((local_tokens, rest), jnp.float32)], axis=1
    )
    both = 2 * kv_cols
    rest = (both + 127) // 128 * 128 - groups * HD
    key_tables = (
        jnp.concatenate(
            [cosine] * (2 * groups) + [jnp.ones((local_tokens, rest), jnp.float32)], axis=1
        ),
        jnp.concatenate(
            [-sine, nothing] * groups + [jnp.zeros((local_tokens, rest), jnp.float32)], axis=1
        ),
        jnp.concatenate(
            [nothing, sine] * groups + [jnp.zeros((local_tokens, rest), jnp.float32)], axis=1
        ),
    )
    cos_tall = jnp.concatenate([cosine.T] * per, axis=1)
    sin_tall = jnp.concatenate([sine.T] * per, axis=1)
    slots = jnp.concatenate([query_slots] * per)[None]

    flat = tokens.reshape(rows, width)
    input_one, query_rot, kv = project(
        flat, gain_attn, full_qkv, cos_wide, ahead, behind, micro_count, q_cols, 2 * kv_cols
    )

    def piece_of(array, piece):
        return array[piece * piece_rows : (piece + 1) * piece_rows]

    live = (query_slots[None, None, :] < lengths[:, :, None]).reshape(rows, 1)
    grad_out = jnp.where(live, cotangent.reshape(rows, width), 0)

    metas = [
        jnp.concatenate([me.astype(jnp.int32)[None], lengths[piece]]) for piece in pieces
    ]
    bits = chip_bits()
    keys = [
        cube_gather(piece_of(kv, piece), bits if piece % 2 == 0 else bits[::-1])
        for piece in pieces
    ]

    def attend_piece(piece, *others):
        own, other = keys[piece]
        query = after(piece_of(query_rot, piece), *others)
        att, lse = attend(metas[piece], slots, query, own, other, groups, window)
        return att, lse, dot(att, full_out, 1, 1).astype(LOW)

    def residual(piece, summed):
        piece_tokens = take_chunk(piece_of(flat, piece), place, chunk).astype(jnp.float32)
        hidden = piece_tokens + summed
        scale = norm_scale(hidden)
        normed = hidden * scale
        return hidden, scale, normed, (normed * gain_ffn).astype(LOW)

    def hidden_back(piece, grad_two, kept):
        _, scale, normed, _ = kept
        gain_term = jnp.sum(grad_two * normed, axis=0)
        grad_hidden = take_chunk(piece_of(grad_out, piece), place, chunk).astype(
            jnp.float32
        ) + norm_back(grad_two, gain_ffn, normed, scale)
        return gain_term, grad_hidden, grad_hidden.astype(LOW)

    def scatter_weight(term):
        return lax.psum_scatter(term, "ctx", scatter_dimension=0, tiled=True)

    def weight_grad(left, right, *others):
        term = dot(after(left, *others), right, 0, 0).astype(LOW)
        return with_layout_constraint(term, Layout((0, 1)))

    def attention_back(piece, grad_low, *others):
        grad_att = dot(after(grad_low, *others), full_out, 1, 0).astype(LOW)
        own, other = keys[piece]
        return attend_back(
            metas[piece], slots, cos_tall, sin_tall, piece_of(query_rot, piece), own, other,
            atts[piece], grad_att, lses[piece], groups, window,
        )

    def one_back(back, *others):
        return dot(after(back, *others), full_qkv[:, :used], 1, 1).astype(LOW)

    def tokens_back(piece, grad_one, grad_hidden):
        piece_tokens = take_chunk(piece_of(flat, piece), place, chunk).astype(jnp.float32)
        scale = norm_scale(piece_tokens)
        normed = piece_tokens * scale
        gain_term = jnp.sum(grad_one * normed, axis=0)
        total = grad_hidden + norm_back(grad_one, gain_attn, normed, scale)
        return gain_term, total.astype(LOW)

    att0, lse0, branch0 = attend_piece(0)
    sum0 = ChainScatter(branch0)
    sum0.next()
    att1, lse1, branch1 = attend_piece(1, branch0)
    atts, lses = (att0, att1), (lse0, lse1)
    sum1 = ChainScatter(branch1, *sum0.landed)
    kept0 = residual(0, sum0.finish())
    two0 = ChainGather(kept0[3])
    sum1.next()
    two0.next()
    two0.next(full_gate, full_up)
    kept1 = residual(1, sum1.finish())
    two1 = ChainGather(kept1[3])
    input0 = two0.finish()

    act0, grad_gate0, grad_up0 = feed(
        after(input0, kept1[3]), piece_of(grad_out, 0), full_gate, full_up, full_down
    )
    two1.next(full_down)
    back_two0 = back_through((after(grad_gate0, two1.landed), grad_up0), (full_gate, full_up))
    back_sum0 = Scatter(back_two0)
    input1 = two1.finish()
    act1, grad_gate1, grad_up1 = feed(
        after(input1, back_two0), piece_of(grad_out, 1), full_gate, full_up, full_down
    )
    back_sum0.next(act1)
    back_two1 = back_through((grad_gate1, grad_up1), (full_gate, full_up))
    back_sum1 = Scatter(back_two1)
    acts = jnp.concatenate([act0, act1], axis=0)
    ffn = back_through((after(acts, back_two1),), (full_down,))
    gain0, grad_hidden0, low0 = hidden_back(0, back_sum0.finish(back_two1), kept0)
    hidden0 = Gather(low0)
    down_term = weight_grad(grad_out, acts, ffn, back_sum1.landed)
    down_grad = scatter_weight(down_term)
    back_sum1.next()
    input_two = jnp.concatenate([input0, input1], axis=0)
    gate_term = weight_grad(
        input_two, jnp.concatenate([grad_gate0, grad_gate1], axis=0), down_term, hidden0.landed
    )
    gate_grad = scatter_weight(gate_term)
    hidden0.next()
    up_term = weight_grad(
        input_two, jnp.concatenate([grad_up0, grad_up1], axis=0), gate_term, back_sum1.landed
    )
    up_grad = scatter_weight(up_term)
    gain1, grad_hidden1, low1 = hidden_back(1, back_sum1.finish(), kept1)
    hidden1 = Gather(low1)
    whole0 = hidden0.finish()
    mixed0 = Scatter(piece_of(ffn, 0), whole0)
    query0, own0, other0 = attention_back(0, whole0, low1, up_term)
    keys0 = Reduce(own0, other0, bits)
    hidden1.next()
    mixed1 = Scatter(piece_of(ffn, 1), hidden1.landed)
    whole1 = hidden1.finish()
    query1, own1, other1 = attention_back(1, whole1, query0, mixed0.landed)
    mixed0.next()
    keys1 = Reduce(own1, other1, bits)
    keys0.next()
    keys1.next()
    out_term = weight_grad(
        jnp.concatenate([whole0, whole1], axis=0),
        jnp.concatenate([att0, att1], axis=0),
        query1,
        mixed1.landed,
        gate_grad,
    )
    out_grad = scatter_weight(out_term)
    mixed1.next()
    back0 = join_back(query0, *keys0.finish(), *key_tables)
    back_one0 = one_back(back0, out_term, mixed0.landed)
    one0 = Scatter(back_one0)
    whole_mixed0 = Gather((kept0[0] + mixed0.finish()).astype(LOW))
    back1 = join_back(query1, *keys1.finish(), *key_tables)
    back_one1 = one_back(back1, back_one0, mixed1.landed)
    one1 = Scatter(back_one1, one0.landed)
    qkv_term = weight_grad(input_one, jnp.concatenate([back0, back1], axis=0), back_one1, up_grad)
    qkv_grad = scatter_weight(qkv_term).astype(jnp.float32)
    whole_mixed1 = Gather((kept1[0] + mixed1.finish()).astype(LOW), qkv_term)
    one0.next()
    whole_mixed0.next()
    gain2, total0 = tokens_back(0, one0.finish(), grad_hidden0)
    tokens0 = Gather(total0)
    one1.next()
    whole_mixed1.next()
    tokens0.next()
    gain3, total1 = tokens_back(1, one1.finish(), grad_hidden1)
    tokens1 = Gather(total1)
    mixed_parts = [whole_mixed0.finish(), whole_mixed1.finish()]
    token_parts = [tokens0.finish(), tokens1.finish()]
    gain_terms = jnp.stack([gain2 + gain3, gain0 + gain1])
    for bit in line_bits():
        gain_terms = gain_terms + line_swap(gain_terms, bit)
    gain_terms = jnp.swapaxes(
        gain_terms.reshape(2, lax.axis_size("ctx"), attn_gain.shape[0]), 0, 1
    )
    for bit in (bits[::-1] + [1]):
        half = gain_terms.shape[0] // 2
        mine = lax.rem(me // bit, 2)
        got = lax.ppermute(take_chunk(gain_terms, 1 - mine, half), "ctx", flip(bit))
        gain_terms = take_chunk(gain_terms, mine, half) + got
    gain_terms = gain_terms[0]
    mixed = jnp.stack(mixed_parts, axis=0).reshape(tokens.shape)
    token_grad = jnp.stack(token_parts, axis=0).reshape(tokens.shape).astype(jnp.float32)
    return (
        mixed,
        token_grad,
        gain_terms[0],
        qkv_grad[:, :q_cols],
        qkv_grad[:, q_cols : q_cols + kv_cols],
        qkv_grad[:, q_cols + kv_cols :],
        out_grad.T.astype(jnp.float32),
        gain_terms[1],
        gate_grad.astype(jnp.float32),
        up_grad.astype(jnp.float32),
        down_grad.T.astype(jnp.float32),
    )


def solution(mesh):
    placed = (
        P(None, None, "ctx", None),
        P(),
        P(None, None, "ctx", None),
        P("ctx"),
        P("ctx", "head"),
        P("ctx", "head"),
        P("ctx", "head"),
        P("head", "ctx"),
        P("ctx"),
        P("ctx", "head"),
        P("ctx", "head"),
        P("head", "ctx"),
    )
    return jax.shard_map(
        per_device,
        mesh=mesh,
        in_specs=placed,
        out_specs=(
            P(None, None, "ctx", None),
            P(None, None, "ctx", None),
            P("ctx"),
            P("ctx", "head"),
            P("ctx", "head"),
            P("ctx", "head"),
            P("head", "ctx"),
            P("ctx"),
            P("ctx", "head"),
            P("ctx", "head"),
            P("head", "ctx"),
        ),
        check_vma=False,
    )
```

```python
import functools

import jax
import jax.numpy as jnp
from jax import lax
from jax.experimental.layout import Layout, with_layout_constraint
from jax.experimental import pallas as pl
from jax.experimental.pallas import tpu as pltpu
from jax.sharding import PartitionSpec as P

HD = 80
WINDOW = 4096

EPSILON = 1e-05
THETA_BASE = 10000.0
NEGATIVE = -1e30
LOG2E = 1.4426950408889634
LOW = jnp.bfloat16
VMEM_LIMIT = 48 * 1024 * 1024
COST = 2


def dot(left, right, a, b):
    return lax.dot_general(
        left, right, (((a,), (b,)), ((), ())), preferred_element_type=jnp.float32
    )


def after(value, *others):
    if not others:
        return value
    return lax.optimization_barrier((value, others))[0]


def angles(positions):
    half = HD // 2
    freq = THETA_BASE ** (-jnp.arange(half, dtype=jnp.float32) * 2.0 / HD)
    angle = positions.astype(jnp.float32)[:, None] * freq[None, :]
    return jnp.cos(angle), jnp.sin(angle)


def add_low(*terms):
    return sum(term.astype(jnp.float32) for term in terms).astype(LOW)


def flip(bit):
    n = lax.axis_size("ctx")
    return [(i, i ^ bit) for i in range(n)]


def chip_bits():
    bits, bit = [], 2
    while bit < lax.axis_size("ctx"):
        bits.append(bit)
        bit *= 2
    return bits


def cube_gather(part, bits):
    own, places = part[None], [0]
    for bit in bits:
        got = lax.ppermute(own, "ctx", flip(bit))
        own = jnp.concatenate([own, got], axis=0)
        places = places + [place ^ (bit // 2) for place in places]
    order = [places.index(m) for m in range(len(places))]
    if order != sorted(order):
        own = jnp.stack([own[at] for at in order], axis=0)
    return own, lax.ppermute(own, "ctx", flip(1))


def line_bits():
    bits, bit = [], 1
    while bit < lax.axis_size("head"):
        bits.append(bit)
        bit *= 2
    return bits


def line_swap(value, bit):
    n = lax.axis_size("head")
    return lax.ppermute(value, "head", [(i, i ^ bit) for i in range(n)])


def line_place(z):
    place = z * 0
    for bit in line_bits():
        place = place * 2 + lax.rem(z // bit, 2)
    return place


class Scatter:
    def __init__(self, partial, *others):
        self.held = after(partial, *others)
        self.bits = line_bits()
        self.send()

    def send(self):
        half = self.held.shape[0] // 2
        mine = lax.rem(lax.axis_index("head") // self.bits[0], 2)
        self.landed = line_swap(
            take_chunk(self.held, 1 - mine, half).astype(LOW), self.bits[0]
        )
        self.kept = take_chunk(self.held, mine, half).astype(jnp.float32)
        self.bits = self.bits[1:]

    def land(self):
        self.held = self.kept + self.landed.astype(jnp.float32)

    def next(self, *others):
        self.landed = after(self.landed, *others)
        self.land()
        self.send()
        return self

    def finish(self, *others):
        while self.bits:
            self.next()
        self.landed = after(self.landed, *others)
        self.land()
        return self.held


class Gather:
    def __init__(self, chunk, *others):
        self.held = after(chunk, *others)
        self.bits = line_bits()[::-1]
        self.send()

    def send(self):
        self.mine = lax.rem(lax.axis_index("head") // self.bits[0], 2)
        self.landed = line_swap(self.held, self.bits[0])
        self.bits = self.bits[1:]

    def land(self):
        first = jnp.where(self.mine == 0, self.held, self.landed)
        second = jnp.where(self.mine == 0, self.landed, self.held)
        self.held = jnp.concatenate([first, second], axis=0)

    def next(self, *others):
        self.landed = after(self.landed, *others)
        self.land()
        self.send()
        return self

    def finish(self, *others):
        while self.bits:
            self.next()
        self.landed = after(self.landed, *others)
        self.land()
        return self.held


class ChainScatter:
    def __init__(self, partial, *others):
        self.partial = self.held = after(partial, *others)
        self.step = 0
        self.send()

    def block(self, z):
        n = lax.axis_size("head")
        size = self.partial.shape[0] // n
        return take_chunk(self.partial, line_place(jnp.clip(z, 0, n - 1)), size)

    def send(self):
        n = lax.axis_size("head")
        z = lax.axis_index("head")
        step = self.step
        rising = self.block(n - 1 - step + z)
        falling = self.block(step + z - (n - 1))
        if step:
            rising = add_low(rising, self.landed[0])
            falling = add_low(falling, self.landed[1])
        self.landed = (
            lax.ppermute(rising, "head", [(i, i + 1) for i in range(step + 1)]),
            lax.ppermute(falling, "head", [(i, i - 1) for i in range(n - 1 - step, n)]),
        )
        self.step += 1

    def next(self, *others):
        self.landed = (after(self.landed[0], *others), self.landed[1])
        self.send()
        return self

    def finish(self, *others):
        while self.step < lax.axis_size("head") - 1:
            self.next()
        mine = after(self.block(lax.axis_index("head")), *others)
        return sum(part.astype(jnp.float32) for part in (mine,) + self.landed)


class ChainGather:
    def __init__(self, chunk, *others):
        self.chunk = after(chunk, *others)
        self.landed = (self.chunk, self.chunk)
        self.got = []
        self.send()

    def send(self):
        n = lax.axis_size("head")
        step = len(self.got)
        self.landed = (
            lax.ppermute(self.landed[0], "head", [(i, i + 1) for i in range(step, n - 1)]),
            lax.ppermute(self.landed[1], "head", [(i, i - 1) for i in range(1, n - step)]),
        )
        self.got.append(self.landed)

    def next(self, *others):
        self.landed = (after(self.landed[0], *others), self.landed[1])
        self.send()
        return self

    def finish(self, *others):
        n = lax.axis_size("head")
        z = lax.axis_index("head")
        while len(self.got) < n - 1:
            self.next()
        size = self.chunk.shape[0]
        whole = jnp.zeros((n * size,) + self.chunk.shape[1:], self.chunk.dtype)
        whole = lax.dynamic_update_slice_in_dim(
            whole, after(self.chunk, *others), line_place(z) * size, axis=0
        )
        for step in range(n - 1):
            block = jnp.where(z > step, self.got[step][0], self.got[n - 2 - step][1])
            at = line_place(lax.rem(z - 1 - step + n, n)) * size
            whole = lax.dynamic_update_slice_in_dim(whole, block, at, axis=0)
        return whole


class Reduce:
    def __init__(self, own, other, bits):
        self.bits = bits[::-1]
        self.kept = own
        self.landed = lax.ppermute(other, "ctx", flip(1))

    def next(self, *others):
        landed = after(self.landed, *others)
        bit, self.bits = self.bits[0], self.bits[1:]
        half = self.kept.shape[0] // 2
        sent = add_low(self.kept[half:], landed[half:])
        self.kept = add_low(self.kept[:half], landed[:half])
        self.sent = sent
        self.landed = lax.ppermute(sent, "ctx", flip(bit))

    def finish(self):
        while self.bits:
            self.next()
        return self.kept[0], self.landed[0]


def project_kernel(tokens_ref, gain_ref, weight_ref, cos_ref, ahead_ref, behind_ref, normed_ref, query_ref, kv_ref):
    values = tokens_ref[...].astype(jnp.float32)
    scale = lax.rsqrt(jnp.mean(values * values, axis=-1, keepdims=True) + EPSILON)
    normed = (values * scale * gain_ref[...]).astype(LOW)
    normed_ref[...] = normed
    out = dot(normed, weight_ref[...], 1, 0)
    local, padded = cos_ref.shape
    q_cols, kv_cols = query_ref.shape[1], kv_ref.shape[1]
    for start in range(0, out.shape[0], local):
        part = out[start : start + local]
        turned = (
            part * cos_ref[...]
            + pltpu.roll(part, padded - HD // 2, 1) * ahead_ref[...]
            + pltpu.roll(part, HD // 2, 1) * behind_ref[...]
        ).astype(LOW)
        query_ref[start : start + local, :] = turned[:, :q_cols]
        kv_ref[start : start + local, :] = turned[:, q_cols : q_cols + kv_cols]


def project(flat, gain, weight, cos, ahead, behind, pieces, q_cols, kv_cols):
    rows, width = flat.shape
    size = rows // pieces
    padded = weight.shape[1]
    whole = lambda shape: pl.BlockSpec(shape, lambda i: (0,) * len(shape))
    strip = lambda columns: pl.BlockSpec((size, columns), lambda i: (i, 0))
    return pl.pallas_call(
        project_kernel,
        grid=(pieces,),
        in_specs=[
            strip(width),
            whole((1, width)),
            whole((width, padded)),
            whole(cos.shape),
            whole(cos.shape),
            whole(cos.shape),
        ],
        out_specs=[strip(width), strip(q_cols), strip(kv_cols)],
        out_shape=[
            jax.ShapeDtypeStruct((rows, width), LOW),
            jax.ShapeDtypeStruct((rows, q_cols), LOW),
            jax.ShapeDtypeStruct((rows, kv_cols), LOW),
        ],
        compiler_params=pltpu.CompilerParams(vmem_limit_bytes=VMEM_LIMIT),
        cost_estimate=pl.CostEstimate(
            flops=2 * rows * width * padded,
            bytes_accessed=4 * rows * width + 2 * width * padded,
            transcendentals=0,
        ),
        name="project",
    )(flat, gain, weight, cos, ahead, behind)


def feed_kernel(input_ref, grad_ref, gate_ref, up_ref, down_ref, act_ref, grad_gate_ref, grad_up_ref):
    gate = dot(input_ref[...], gate_ref[...], 1, 0)
    up = dot(input_ref[...], up_ref[...], 1, 0)
    grad_act = dot(grad_ref[...], down_ref[...], 1, 0)
    sigmoid = jax.nn.sigmoid(gate)
    silu = gate * sigmoid
    act_ref[...] = (silu * up).astype(LOW)
    grad_gate_ref[...] = (grad_act * up * sigmoid * (1.0 + gate * (1.0 - sigmoid))).astype(LOW)
    grad_up_ref[...] = (grad_act * silu).astype(LOW)


def feed(inputs, grads, gate, up, down):
    rows, width = inputs.shape
    units = gate.shape[1]
    tile = 256
    whole = pl.BlockSpec((rows, width), lambda i: (0, 0))
    weight = pl.BlockSpec((width, tile), lambda i: (0, i))
    out = pl.BlockSpec((rows, tile), lambda i: (0, i))
    return pl.pallas_call(
        feed_kernel,
        grid=((units + tile - 1) // tile,),
        in_specs=[whole, whole, weight, weight, weight],
        out_specs=[out, out, out],
        out_shape=[jax.ShapeDtypeStruct((rows, units), LOW)] * 3,
        compiler_params=pltpu.CompilerParams(vmem_limit_bytes=VMEM_LIMIT),
        cost_estimate=pl.CostEstimate(
            flops=6 * rows * width * units // COST,
            bytes_accessed=(6 * width * units + 4 * rows * width + 6 * rows * units) // COST,
            transcendentals=0,
        ),
        name="feed",
    )(inputs, grads, gate, up, down)


def back_kernel(*refs):
    out_ref = refs[-1]
    count = (len(refs) - 1) // 2
    total = dot(refs[0][...], refs[count][...], 1, 1)
    for at in range(1, count):
        total += dot(refs[at][...], refs[count + at][...], 1, 1)
    out_ref[...] = total.astype(LOW)


def back_through(values, weights):
    rows, units = values[0].shape
    width = weights[0].shape[0]
    tile = 256
    count = len(values)
    return pl.pallas_call(
        back_kernel,
        grid=((width + tile - 1) // tile,),
        in_specs=[pl.BlockSpec((rows, units), lambda i: (0, 0))] * count
        + [pl.BlockSpec((tile, units), lambda i: (i, 0))] * count,
        out_specs=pl.BlockSpec((rows, tile), lambda i: (0, i)),
        out_shape=jax.ShapeDtypeStruct((rows, width), LOW),
        compiler_params=pltpu.CompilerParams(vmem_limit_bytes=VMEM_LIMIT),
        cost_estimate=pl.CostEstimate(
            flops=2 * count * rows * width * units // COST,
            bytes_accessed=(2 * count * (width + rows) * units + 2 * rows * width) // COST,
            transcendentals=0,
        ),
        name="back_through",
    )(*values, *weights)


def join_kernel(query_ref, kept_ref, landed_ref, cos_ref, ahead_ref, behind_ref, out_ref):
    q_cols, kv_cols = query_ref.shape[1], kept_ref.shape[1]
    local, padded = cos_ref.shape
    out_ref[:, :q_cols] = query_ref[...]
    for start in range(0, kept_ref.shape[0], local):
        rows = slice(start, start + local)
        part = kept_ref[rows, :].astype(jnp.float32) + landed_ref[rows, :].astype(jnp.float32)
        if padded > kv_cols:
            part = jnp.concatenate(
                [part, jnp.zeros((local, padded - kv_cols), jnp.float32)], axis=1
            )
        turned = (
            part * cos_ref[...]
            - pltpu.roll(part, padded - HD // 2, 1) * ahead_ref[...]
            - pltpu.roll(part, HD // 2, 1) * behind_ref[...]
        ).astype(LOW)
        out_ref[rows, q_cols : q_cols + kv_cols] = turned[:, :kv_cols]


def join_back(query, kept, landed, cos, ahead, behind):
    rows, q_cols = query.shape
    return pl.pallas_call(
        join_kernel,
        out_shape=jax.ShapeDtypeStruct((rows, q_cols + kept.shape[1]), LOW),
        compiler_params=pltpu.CompilerParams(vmem_limit_bytes=VMEM_LIMIT),
        cost_estimate=pl.CostEstimate(flops=0, bytes_accessed=8 * kept.size, transcendentals=0),
        name="join_back",
    )(query, kept, landed, cos, ahead, behind)


def stack_heads(block, group, per):
    return jnp.concatenate(
        [block[:, (group * per + h) * HD : (group * per + h + 1) * HD] for h in range(per)],
        axis=0,
    )


def key_block(own_ref, other_ref, at, column):
    return jnp.concatenate(
        [own_ref[at, :, column : column + HD], other_ref[at, :, column : column + HD]],
        axis=0,
    )


def key_limits(meta_ref, slots_ref, local):
    me, length = meta_ref[0], meta_ref[1 + pl.program_id(0)]
    pair = 2 * local
    full = lax.div(jnp.minimum(me * local + 1, length), pair)
    some = lax.div(jnp.minimum((me + 1) * local, length) + pair - 1, pair)
    limit = jnp.minimum(slots_ref[...], length - 1)
    row = lax.broadcasted_iota(jnp.int32, (pair, 1), 0)
    core = lax.rem(me, 2)
    within = jnp.where(row < local, core * local + row, (1 - core) * local + row - local)
    return me, length, full, some, limit, within


def keep_allowed(scores, base, within, limit, slots, window):
    place = base + within
    allowed = place <= limit
    if window:
        allowed = allowed & (slots - place < WINDOW)
    return jnp.where(allowed, scores, NEGATIVE)


def attend_kernel(meta_ref, slots_ref, query_ref, own_ref, other_ref, att_ref, lse_ref, stacked, total, *, groups, per, window):
    local = query_ref.shape[0]
    pair = 2 * local
    kv_cols = groups * HD
    me, _, full, some, limit, within = key_limits(meta_ref, slots_ref, local)
    if window:
        full = full * 0
    factor = HD ** (-0.5) * LOG2E
    for g in range(groups):
        stacked[g] = stack_heads(query_ref[...], g, per)
        total[g] = jnp.zeros(total.shape[1:], jnp.float32)

    def step(m, carry, masked):
        at = jnp.bitwise_xor(m, lax.div(me, 2))
        out = []
        for g in range(groups):
            top, weight = carry[g]
            keys = key_block(own_ref, other_ref, at, g * HD)
            values = key_block(own_ref, other_ref, at, kv_cols + g * HD)
            scores = dot(keys, stacked[g], 1, 1) * factor
            if masked:
                scores = keep_allowed(scores, m * pair, within, limit, slots_ref[...], window)
            higher = jnp.maximum(top, jnp.max(scores, axis=0, keepdims=True))
            probs = jnp.exp2(scores - higher)
            shrink = jnp.exp2(top - higher)
            total[g] = total[g] * shrink + dot(values, probs.astype(LOW), 0, 0)
            out.append(
                (higher, weight * shrink + jnp.sum(probs, axis=0, keepdims=True))
            )
        return tuple(out)

    row = (1, per * local)
    carry = tuple(
        (jnp.full(row, NEGATIVE, jnp.float32), jnp.zeros(row, jnp.float32))
        for _ in range(groups)
    )
    carry = lax.fori_loop(0, full, lambda m, c: step(m, c, False), carry)
    carry = lax.fori_loop(full, some, lambda m, c: step(m, c, True), carry)
    for g in range(groups):
        top, weight = carry[g]
        lse_ref[0, g : g + 1, :] = top + jnp.log2(weight)
        out = (total[g] / weight).T.astype(LOW)
        for h in range(per):
            at = (g * per + h) * HD
            att_ref[:, at : at + HD] = out[h * local : (h + 1) * local]


def attend_back_kernel(
    meta_ref, slots_ref, cos_ref, sin_ref, query_ref, own_ref, other_ref, att_ref, grad_ref, lse_ref,
    grad_query_ref, grad_own_ref, grad_other_ref, stacked, stacked_grad, total, row_dot, *, groups, per, window,
):
    local = query_ref.shape[0]
    pair = 2 * local
    kv_cols = groups * HD
    me, length, full, some, limit, within = key_limits(meta_ref, slots_ref, local)
    if window:
        full = full * 0
    scale = HD ** (-0.5)
    live = me * local < length
    full = jnp.where(live, full, 0)
    some = jnp.where(live, some, 0)
    chips = own_ref.shape[0]
    chip = lax.div(me, 2)

    for g in range(groups):
        stacked[g] = stack_heads(query_ref[...], g, per)
        grads = stack_heads(grad_ref[...], g, per)
        stacked_grad[g] = grads
        product = grads.astype(jnp.float32) * stack_heads(att_ref[...], g, per).astype(jnp.float32)
        row_dot[g : g + 1, :] = jnp.sum(product.T, axis=0, keepdims=True)
        total[g] = jnp.zeros(total.shape[1:], jnp.float32)

    def clear(m, carry):
        at = jnp.bitwise_xor(m, chip)
        grad_own_ref[at] = jnp.zeros(grad_own_ref.shape[1:], LOW)
        grad_other_ref[at] = jnp.zeros(grad_other_ref.shape[1:], LOW)
        return carry

    def step(m, carry, masked):
        at = jnp.bitwise_xor(m, chip)
        for g in range(groups):
            keys = key_block(own_ref, other_ref, at, g * HD)
            values = key_block(own_ref, other_ref, at, kv_cols + g * HD)
            scores = dot(keys, stacked[g], 1, 1) * (scale * LOG2E)
            if masked:
                scores = keep_allowed(scores, m * pair, within, limit, slots_ref[...], window)
            probs = jnp.exp2(scores - lse_ref[0, g : g + 1, :])
            grad_probs = dot(values, stacked_grad[g], 1, 1)
            grad_scores = (probs * (grad_probs - row_dot[g : g + 1, :])).astype(LOW)
            grad_values = dot(probs.astype(LOW), stacked_grad[g], 1, 0).astype(LOW)
            grad_keys = (dot(grad_scores, stacked[g], 1, 0) * scale).astype(LOW)
            total[g] += dot(keys, grad_scores, 0, 0)
            for column, grads in ((g * HD, grad_keys), (kv_cols + g * HD, grad_values)):
                grad_own_ref[at, :, column : column + HD] = grads[:local]
                grad_other_ref[at, :, column : column + HD] = grads[local:]
        return carry

    lax.fori_loop(0, full, lambda m, c: step(m, c, False), 0)
    lax.fori_loop(full, some, lambda m, c: step(m, c, True), 0)
    lax.fori_loop(some, chips, clear, 0)
    half = HD // 2
    cos, sin = cos_ref[...], sin_ref[...]
    for g in range(groups):
        grads = total[g] * scale
        first, second = grads[:half], grads[half:]
        turned = jnp.concatenate(
            [first * cos + second * sin, second * cos - first * sin], axis=0
        ).T.astype(LOW)
        for h in range(per):
            at = (g * per + h) * HD
            grad_query_ref[:, at : at + HD] = turned[h * local : (h + 1) * local]


def attention_specs(seqs, local, q_cols, kv_both, chips, groups, columns):
    meta = pl.BlockSpec(memory_space=pltpu.SMEM)
    whole = lambda shape: pl.BlockSpec(shape, lambda s: (0,) * len(shape))
    queries = pl.BlockSpec((local, q_cols), lambda s: (s, 0))
    keys = pl.BlockSpec((chips, local, kv_both), lambda s: (0, s, 0))
    lse = pl.BlockSpec((1, groups, columns), lambda s: (s, 0, 0))
    return meta, whole, queries, keys, lse


def attend(meta, slots, query, own, other, groups, window):
    seqs = meta.shape[0] - 1
    rows, q_cols = query.shape
    local = rows // seqs
    chips, _, kv_both = own.shape
    per = q_cols // HD // groups
    columns = per * local
    smem, whole, queries, keys, lse = attention_specs(
        seqs, local, q_cols, kv_both, chips, groups, columns
    )
    pairs = rows * q_cols // HD * 2 * chips * local
    return pl.pallas_call(
        functools.partial(attend_kernel, groups=groups, per=per, window=window),
        grid=(seqs,),
        in_specs=[smem, whole((1, columns)), queries, keys, keys],
        out_specs=[queries, lse],
        out_shape=[
            jax.ShapeDtypeStruct((rows, q_cols), LOW),
            jax.ShapeDtypeStruct((seqs, groups, columns), jnp.float32),
        ],
        scratch_shapes=[
            pltpu.VMEM((groups, columns, HD), LOW),
            pltpu.VMEM((groups, HD, columns), jnp.float32),
        ],
        compiler_params=pltpu.CompilerParams(vmem_limit_bytes=VMEM_LIMIT),
        cost_estimate=pl.CostEstimate(
            flops=12 * pairs * HD // COST, bytes_accessed=4 * own.size // COST, transcendentals=0
        ),
        name="attend",
    )(meta, slots, query, own, other)


def attend_back(meta, slots, cos, sin, query, own, other, att, grad, lse_rows, groups, window):
    seqs = meta.shape[0] - 1
    rows, q_cols = query.shape
    local = rows // seqs
    chips, _, kv_both = own.shape
    per = q_cols // HD // groups
    columns = per * local
    smem, whole, queries, keys, lse = attention_specs(
        seqs, local, q_cols, kv_both, chips, groups, columns
    )
    pairs = rows * q_cols // HD * 2 * chips * local
    return pl.pallas_call(
        functools.partial(attend_back_kernel, groups=groups, per=per, window=window),
        grid=(seqs,),
        in_specs=[
            smem, whole((1, columns)), whole(cos.shape), whole(cos.shape),
            queries, keys, keys, queries, queries, lse,
        ],
        out_specs=[queries, keys, keys],
        out_shape=[
            jax.ShapeDtypeStruct((rows, q_cols), LOW),
            jax.ShapeDtypeStruct(own.shape, LOW),
            jax.ShapeDtypeStruct(own.shape, LOW),
        ],
        scratch_shapes=[
            pltpu.VMEM((groups, columns, HD), LOW),
            pltpu.VMEM((groups, columns, HD), LOW),
            pltpu.VMEM((groups, HD, columns), jnp.float32),
            pltpu.VMEM((groups, columns), jnp.float32),
        ],
        compiler_params=pltpu.CompilerParams(vmem_limit_bytes=VMEM_LIMIT),
        cost_estimate=pl.CostEstimate(
            flops=30 * pairs * HD // COST, bytes_accessed=8 * own.size // COST, transcendentals=0
        ),
        name="attend_back",
    )(meta, slots, cos, sin, query, own, other, att, grad, lse_rows)


def take_chunk(rows, index, size):
    return lax.dynamic_slice_in_dim(rows, index * size, size, axis=0)


def norm_scale(values):
    return lax.rsqrt(jnp.mean(values * values, axis=-1, keepdims=True) + EPSILON)


def norm_back(grad, gain, normed, scale):
    scaled = grad * gain
    return scale * (scaled - normed * jnp.mean(scaled * normed, axis=-1, keepdims=True))


def per_device(
    tokens,
    lengths,
    cotangent,
    attn_gain,
    query_weight,
    key_weight,
    value_weight,
    out_weight,
    ffn_gain,
    gate_weight,
    up_weight,
    down_weight,
):
    micro_count, seq_count, local_tokens, width = tokens.shape
    place = line_place(lax.axis_index("head"))
    me = lax.axis_index("ctx")
    lines = lax.axis_size("head")
    q_cols = query_weight.shape[1]
    kv_cols = key_weight.shape[1]
    used = q_cols + 2 * kv_cols
    padded = (used + 2 + 127) // 128 * 128

    qkv_shard = jnp.concatenate(
        [
            query_weight,
            key_weight,
            value_weight,
            attn_gain[:, None],
            ffn_gain[:, None],
            jnp.zeros((query_weight.shape[0], padded - used - 2), LOW),
        ],
        axis=1,
    )
    full_qkv = lax.all_gather(qkv_shard, "ctx", axis=0, tiled=True)
    full_out = lax.all_gather(out_weight.T, "ctx", axis=0, tiled=True)
    full_gate = lax.all_gather(gate_weight, "ctx", axis=0, tiled=True)
    full_up = lax.all_gather(up_weight, "ctx", axis=0, tiled=True)
    full_down = lax.all_gather(down_weight.T, "ctx", axis=0, tiled=True)
    gains = full_qkv[:, used : used + 2].T.astype(jnp.float32)
    gain_attn = gains[0:1]
    gain_ffn = gains[1:2]

    heads = q_cols // HD
    groups = kv_cols // HD
    per = heads // groups
    span_total = local_tokens * lax.axis_size("ctx")
    window = span_total > WINDOW
    query_slots = me * local_tokens + jnp.arange(local_tokens, dtype=jnp.int32)
    cosine, sine = angles(query_slots)
    piece_rows = seq_count * local_tokens
    rows = micro_count * piece_rows
    chunk = piece_rows // lines
    pieces = range(micro_count)

    nothing = jnp.zeros_like(sine)
    turning = heads + groups
    rest = padded - turning * HD
    cos_wide = jnp.concatenate(
        [cosine] * (2 * turning) + [jnp.ones((local_tokens, rest), jnp.float32)], axis=1
    )
    ahead = jnp.concatenate(
        [-sine, nothing] * turning + [jnp.zeros((local_tokens, rest), jnp.float32)], axis=1
    )
    behind = jnp.concatenate(
        [nothing, sine] * turning + [jnp.zeros((local_tokens, rest), jnp.float32)], axis=1
    )
    both = 2 * kv_cols
    rest = (both + 127) // 128 * 128 - groups * HD
    key_tables = (
        jnp.concatenate(
            [cosine] * (2 * groups) + [jnp.ones((local_tokens, rest), jnp.float32)], axis=1
        ),
        jnp.concatenate(
            [-sine, nothing] * groups + [jnp.zeros((local_tokens, rest), jnp.float32)], axis=1
        ),
        jnp.concatenate(
            [nothing, sine] * groups + [jnp.zeros((local_tokens, rest), jnp.float32)], axis=1
        ),
    )
    cos_tall = jnp.concatenate([cosine.T] * per, axis=1)
    sin_tall = jnp.concatenate([sine.T] * per, axis=1)
    slots = jnp.concatenate([query_slots] * per)[None]

    flat = tokens.reshape(rows, width)
    input_one, query_rot, kv = project(
        flat, gain_attn, full_qkv, cos_wide, ahead, behind, micro_count, q_cols, 2 * kv_cols
    )

    def piece_of(array, piece):
        return array[piece * piece_rows : (piece + 1) * piece_rows]

    live = (query_slots[None, None, :] < lengths[:, :, None]).reshape(rows, 1)
    grad_out = jnp.where(live, cotangent.reshape(rows, width), 0)

    metas = [
        jnp.concatenate([me.astype(jnp.int32)[None], lengths[piece]]) for piece in pieces
    ]
    bits = chip_bits()
    keys = [
        cube_gather(piece_of(kv, piece), bits if piece % 2 == 0 else bits[::-1])
        for piece in pieces
    ]

    def attend_piece(piece, *others):
        own, other = keys[piece]
        query = after(piece_of(query_rot, piece), *others)
        att, lse = attend(metas[piece], slots, query, own, other, groups, window)
        return att, lse, dot(att, full_out, 1, 1).astype(LOW)

    def residual(piece, summed):
        piece_tokens = take_chunk(piece_of(flat, piece), place, chunk).astype(jnp.float32)
        hidden = piece_tokens + summed
        scale = norm_scale(hidden)
        normed = hidden * scale
        return hidden, scale, normed, (normed * gain_ffn).astype(LOW)

    def hidden_back(piece, grad_two, kept):
        _, scale, normed, _ = kept
        gain_term = jnp.sum(grad_two * normed, axis=0)
        grad_hidden = take_chunk(piece_of(grad_out, piece), place, chunk).astype(
            jnp.float32
        ) + norm_back(grad_two, gain_ffn, normed, scale)
        return gain_term, grad_hidden, grad_hidden.astype(LOW)

    def scatter_weight(term):
        return lax.psum_scatter(term, "ctx", scatter_dimension=0, tiled=True)

    def weight_grad(left, right, *others):
        term = dot(after(left, *others), right, 0, 0).astype(LOW)
        return with_layout_constraint(term, Layout((0, 1)))

    def attention_back(piece, grad_low, *others):
        grad_att = dot(after(grad_low, *others), full_out, 1, 0).astype(LOW)
        own, other = keys[piece]
        return attend_back(
            metas[piece], slots, cos_tall, sin_tall, piece_of(query_rot, piece), own, other,
            atts[piece], grad_att, lses[piece], groups, window,
        )

    def one_back(back, *others):
        return dot(after(back, *others), full_qkv[:, :used], 1, 1).astype(LOW)

    def tokens_back(piece, grad_one, grad_hidden):
        piece_tokens = take_chunk(piece_of(flat, piece), place, chunk).astype(jnp.float32)
        scale = norm_scale(piece_tokens)
        normed = piece_tokens * scale
        gain_term = jnp.sum(grad_one * normed, axis=0)
        total = grad_hidden + norm_back(grad_one, gain_attn, normed, scale)
        return gain_term, total.astype(LOW)

    att0, lse0, branch0 = attend_piece(0)
    sum0 = ChainScatter(branch0)
    sum0.next()
    att1, lse1, branch1 = attend_piece(1, branch0)
    atts, lses = (att0, att1), (lse0, lse1)
    sum1 = ChainScatter(branch1, *sum0.landed)
    kept0 = residual(0, sum0.finish())
    two0 = ChainGather(kept0[3])
    sum1.next()
    two0.next()
    two0.next(full_gate, full_up)
    kept1 = residual(1, sum1.finish())
    two1 = Gather(kept1[3])
    input0 = two0.finish()

    act0, grad_gate0, grad_up0 = feed(
        after(input0, kept1[3]), piece_of(grad_out, 0), full_gate, full_up, full_down
    )
    two1.next(full_down)
    back_two0 = back_through((after(grad_gate0, two1.landed), grad_up0), (full_gate, full_up))
    back_sum0 = Scatter(back_two0)
    input1 = two1.finish()
    act1, grad_gate1, grad_up1 = feed(
        after(input1, back_two0), piece_of(grad_out, 1), full_gate, full_up, full_down
    )
    back_sum0.next(act1)
    acts = jnp.concatenate([act0, act1], axis=0)
    down_term = weight_grad(grad_out, acts, back_sum0.kept)
    down_grad = scatter_weight(down_term)
    back_two1 = back_through((after(grad_gate1, down_term), grad_up1), (full_gate, full_up))
    gain0, grad_hidden0, low0 = hidden_back(0, back_sum0.finish(back_two1), kept0)
    hidden0 = Gather(low0)
    back_sum1 = Scatter(back_two1)
    ffn = back_through((after(acts, low0, back_two1),), (full_down,))
    input_two = jnp.concatenate([input0, input1], axis=0)
    gate_term = weight_grad(
        input_two,
        jnp.concatenate([grad_gate0, grad_gate1], axis=0),
        ffn,
        back_sum1.landed,
        hidden0.landed,
    )
    gate_grad = scatter_weight(gate_term)
    hidden0.next()
    back_sum1.next()
    up_term = weight_grad(
        input_two, jnp.concatenate([grad_up0, grad_up1], axis=0), gate_term
    )
    up_grad = scatter_weight(up_term)
    whole0 = hidden0.finish(up_term)
    mixed0 = Scatter(piece_of(ffn, 0), whole0)
    gain1, grad_hidden1, low1 = hidden_back(1, back_sum1.finish(up_term), kept1)
    hidden1 = Gather(low1)
    query0, own0, other0 = attention_back(0, whole0, low1)
    keys0 = Reduce(own0, other0, bits)
    hidden1.next()
    keys0.next(mixed0.landed)
    mixed0.next()
    whole1 = hidden1.finish()
    mixed1 = Scatter(piece_of(ffn, 1), whole1)
    whole_mixed0 = Gather((kept0[0] + mixed0.finish()).astype(LOW))
    query1, own1, other1 = attention_back(
        1, whole1, query0, keys0.sent, mixed1.held
    )
    keys1 = Reduce(own1, other1, bits)
    keys0.next(mixed1.landed)
    mixed1.next()
    whole_mixed0.next()
    keys1.next()
    back0 = join_back(query0, *keys0.finish(), *key_tables)
    back_one0 = one_back(back0, query1, keys1.sent)
    one0 = Scatter(back_one0)
    whole_mixed1 = Gather((kept1[0] + mixed1.finish()).astype(LOW))
    keys1.next()
    back1 = join_back(query1, *keys1.finish(), *key_tables)
    back_one1 = one_back(back1, back_one0, one0.held)
    one1 = Scatter(back_one1)
    one0.next()
    whole_mixed1.next()
    last_term = jnp.concatenate(
        [
            weight_grad(
                input_one, jnp.concatenate([back0, back1], axis=0), back_one1, gate_grad
            ),
            weight_grad(
                jnp.concatenate([whole0, whole1], axis=0),
                jnp.concatenate([att0, att1], axis=0),
                back_one1,
            ),
        ],
        axis=1,
    )
    last_grad = scatter_weight(last_term).astype(jnp.float32)
    qkv_grad, out_grad = last_grad[:, :used], last_grad[:, used:]
    gain2, total0 = tokens_back(0, one0.finish(), grad_hidden0)
    tokens0 = ChainGather(total0)
    tokens0_first = tokens0.landed
    one1.next()
    tokens0.next()
    gain3, total1 = tokens_back(1, one1.finish(tokens0_first), grad_hidden1)
    tokens1 = ChainGather(total1)
    mixed_parts = [whole_mixed0.finish(), whole_mixed1.finish()]
    token_parts = [tokens0.finish(), tokens1.finish()]
    gain_terms = after(jnp.stack([gain2 + gain3, gain0 + gain1]), tokens1.landed)
    for bit in line_bits():
        gain_terms = gain_terms + line_swap(gain_terms, bit)
    gain_terms = jnp.swapaxes(
        gain_terms.reshape(2, lax.axis_size("ctx"), attn_gain.shape[0]), 0, 1
    )
    for bit in (bits[::-1] + [1]):
        half = gain_terms.shape[0] // 2
        mine = lax.rem(me // bit, 2)
        got = lax.ppermute(take_chunk(gain_terms, 1 - mine, half), "ctx", flip(bit))
        gain_terms = take_chunk(gain_terms, mine, half) + got
    gain_terms = gain_terms[0]
    mixed = jnp.stack(mixed_parts, axis=0).reshape(tokens.shape)
    token_grad = jnp.stack(token_parts, axis=0).reshape(tokens.shape).astype(jnp.float32)
    return (
        mixed,
        token_grad,
        gain_terms[0],
        qkv_grad[:, :q_cols],
        qkv_grad[:, q_cols : q_cols + kv_cols],
        qkv_grad[:, q_cols + kv_cols :],
        out_grad.T,
        gain_terms[1],
        gate_grad.astype(jnp.float32),
        up_grad.astype(jnp.float32),
        down_grad.T.astype(jnp.float32),
    )


def solution(mesh):
    placed = (
        P(None, None, "ctx", None),
        P(),
        P(None, None, "ctx", None),
        P("ctx"),
        P("ctx", "head"),
        P("ctx", "head"),
        P("ctx", "head"),
        P("head", "ctx"),
        P("ctx"),
        P("ctx", "head"),
        P("ctx", "head"),
        P("head", "ctx"),
    )
    return jax.shard_map(
        per_device,
        mesh=mesh,
        in_specs=placed,
        out_specs=(
            P(None, None, "ctx", None),
            P(None, None, "ctx", None),
            P("ctx"),
            P("ctx", "head"),
            P("ctx", "head"),
            P("ctx", "head"),
            P("head", "ctx"),
            P("ctx"),
            P("ctx", "head"),
            P("ctx", "head"),
            P("head", "ctx"),
        ),
        check_vma=False,
    )
```

```python
import functools

import jax
import jax.numpy as jnp
from jax import lax
from jax.experimental.layout import Layout, with_layout_constraint
from jax.experimental import pallas as pl
from jax.experimental.pallas import tpu as pltpu
from jax.sharding import PartitionSpec as P

HD = 80
WINDOW = 4096

EPSILON = 1e-05
THETA_BASE = 10000.0
NEGATIVE = -1e30
LOG2E = 1.4426950408889634
LOW = jnp.bfloat16
VMEM_LIMIT = 48 * 1024 * 1024
COST = 2


def dot(left, right, a, b):
    return lax.dot_general(
        left, right, (((a,), (b,)), ((), ())), preferred_element_type=jnp.float32
    )


def after(value, *others):
    if not others:
        return value
    return lax.optimization_barrier((value, others))[0]


def angles(positions):
    half = HD // 2
    freq = THETA_BASE ** (-jnp.arange(half, dtype=jnp.float32) * 2.0 / HD)
    angle = positions.astype(jnp.float32)[:, None] * freq[None, :]
    return jnp.cos(angle), jnp.sin(angle)


def add_low(*terms):
    return sum(term.astype(jnp.float32) for term in terms).astype(LOW)


def flip(bit):
    n = lax.axis_size("ctx")
    return [(i, i ^ bit) for i in range(n)]


def chip_bits():
    bits, bit = [], 2
    while bit < lax.axis_size("ctx"):
        bits.append(bit)
        bit *= 2
    return bits


def cube_gather(part, bits):
    own, places = part[None], [0]
    for bit in bits:
        got = lax.ppermute(own, "ctx", flip(bit))
        own = jnp.concatenate([own, got], axis=0)
        places = places + [place ^ (bit // 2) for place in places]
    order = [places.index(m) for m in range(len(places))]
    if order != sorted(order):
        own = jnp.stack([own[at] for at in order], axis=0)
    return own, lax.ppermute(own, "ctx", flip(1))


def line_bits():
    bits, bit = [], 1
    while bit < lax.axis_size("head"):
        bits.append(bit)
        bit *= 2
    return bits


def line_swap(value, bit):
    n = lax.axis_size("head")
    return lax.ppermute(value, "head", [(i, i ^ bit) for i in range(n)])


def line_place(z):
    place = z * 0
    for bit in line_bits():
        place = place * 2 + lax.rem(z // bit, 2)
    return place


class Scatter:
    def __init__(self, partial, *others):
        self.held = after(partial, *others)
        self.bits = line_bits()
        self.send()

    def send(self):
        half = self.held.shape[0] // 2
        mine = lax.rem(lax.axis_index("head") // self.bits[0], 2)
        self.landed = line_swap(
            take_chunk(self.held, 1 - mine, half).astype(LOW), self.bits[0]
        )
        self.kept = take_chunk(self.held, mine, half).astype(jnp.float32)
        self.bits = self.bits[1:]

    def land(self):
        self.held = self.kept + self.landed.astype(jnp.float32)

    def next(self, *others):
        self.landed = after(self.landed, *others)
        self.land()
        self.send()
        return self

    def finish(self, *others):
        while self.bits:
            self.next()
        self.landed = after(self.landed, *others)
        self.land()
        return self.held


class Gather:
    def __init__(self, chunk, *others):
        self.held = after(chunk, *others)
        self.bits = line_bits()[::-1]
        self.send()

    def send(self):
        self.mine = lax.rem(lax.axis_index("head") // self.bits[0], 2)
        self.landed = line_swap(self.held, self.bits[0])
        self.bits = self.bits[1:]

    def land(self):
        first = jnp.where(self.mine == 0, self.held, self.landed)
        second = jnp.where(self.mine == 0, self.landed, self.held)
        self.held = jnp.concatenate([first, second], axis=0)

    def next(self, *others):
        self.landed = after(self.landed, *others)
        self.land()
        self.send()
        return self

    def finish(self, *others):
        while self.bits:
            self.next()
        self.landed = after(self.landed, *others)
        self.land()
        return self.held


class ChainScatter:
    def __init__(self, partial, *others):
        self.partial = self.held = after(partial, *others)
        self.step = 0
        self.send()

    def block(self, z):
        n = lax.axis_size("head")
        size = self.partial.shape[0] // n
        return take_chunk(self.partial, line_place(jnp.clip(z, 0, n - 1)), size)

    def send(self):
        n = lax.axis_size("head")
        z = lax.axis_index("head")
        step = self.step
        rising = self.block(n - 1 - step + z)
        falling = self.block(step + z - (n - 1))
        if step:
            rising = add_low(rising, self.landed[0])
            falling = add_low(falling, self.landed[1])
        self.landed = (
            lax.ppermute(rising, "head", [(i, i + 1) for i in range(step + 1)]),
            lax.ppermute(falling, "head", [(i, i - 1) for i in range(n - 1 - step, n)]),
        )
        self.step += 1

    def next(self, *others):
        self.landed = (after(self.landed[0], *others), self.landed[1])
        self.send()
        return self

    def finish(self, *others):
        while self.step < lax.axis_size("head") - 1:
            self.next()
        mine = after(self.block(lax.axis_index("head")), *others)
        return sum(part.astype(jnp.float32) for part in (mine,) + self.landed)


class ChainGather:
    def __init__(self, chunk, *others):
        self.chunk = after(chunk, *others)
        self.landed = (self.chunk, self.chunk)
        self.got = []
        self.send()

    def send(self):
        n = lax.axis_size("head")
        step = len(self.got)
        self.landed = (
            lax.ppermute(self.landed[0], "head", [(i, i + 1) for i in range(step, n - 1)]),
            lax.ppermute(self.landed[1], "head", [(i, i - 1) for i in range(1, n - step)]),
        )
        self.got.append(self.landed)

    def next(self, *others):
        self.landed = (after(self.landed[0], *others), self.landed[1])
        self.send()
        return self

    def finish(self, *others):
        n = lax.axis_size("head")
        z = lax.axis_index("head")
        while len(self.got) < n - 1:
            self.next()
        size = self.chunk.shape[0]
        whole = jnp.zeros((n * size,) + self.chunk.shape[1:], self.chunk.dtype)
        whole = lax.dynamic_update_slice_in_dim(
            whole, after(self.chunk, *others), line_place(z) * size, axis=0
        )
        for step in range(n - 1):
            block = jnp.where(z > step, self.got[step][0], self.got[n - 2 - step][1])
            at = line_place(lax.rem(z - 1 - step + n, n)) * size
            whole = lax.dynamic_update_slice_in_dim(whole, block, at, axis=0)
        return whole


class Reduce:
    def __init__(self, own, other, bits):
        self.bits = bits[::-1]
        self.kept = own
        self.landed = lax.ppermute(other, "ctx", flip(1))

    def next(self, *others):
        landed = after(self.landed, *others)
        bit, self.bits = self.bits[0], self.bits[1:]
        half = self.kept.shape[0] // 2
        sent = add_low(self.kept[half:], landed[half:])
        self.kept = add_low(self.kept[:half], landed[:half])
        self.sent = sent
        self.landed = lax.ppermute(sent, "ctx", flip(bit))

    def finish(self):
        while self.bits:
            self.next()
        return self.kept[0], self.landed[0]


def project_kernel(tokens_ref, gain_ref, weight_ref, cos_ref, ahead_ref, behind_ref, normed_ref, query_ref, kv_ref):
    values = tokens_ref[...].astype(jnp.float32)
    scale = lax.rsqrt(jnp.mean(values * values, axis=-1, keepdims=True) + EPSILON)
    normed = (values * scale * gain_ref[...]).astype(LOW)
    normed_ref[...] = normed
    out = dot(normed, weight_ref[...], 1, 0)
    local, padded = cos_ref.shape
    q_cols, kv_cols = query_ref.shape[1], kv_ref.shape[1]
    for start in range(0, out.shape[0], local):
        part = out[start : start + local]
        turned = (
            part * cos_ref[...]
            + pltpu.roll(part, padded - HD // 2, 1) * ahead_ref[...]
            + pltpu.roll(part, HD // 2, 1) * behind_ref[...]
        ).astype(LOW)
        query_ref[start : start + local, :] = turned[:, :q_cols]
        kv_ref[start : start + local, :] = turned[:, q_cols : q_cols + kv_cols]


def project(flat, gain, weight, cos, ahead, behind, pieces, q_cols, kv_cols):
    rows, width = flat.shape
    size = rows // pieces
    padded = weight.shape[1]
    whole = lambda shape: pl.BlockSpec(shape, lambda i: (0,) * len(shape))
    strip = lambda columns: pl.BlockSpec((size, columns), lambda i: (i, 0))
    return pl.pallas_call(
        project_kernel,
        grid=(pieces,),
        in_specs=[
            strip(width),
            whole((1, width)),
            whole((width, padded)),
            whole(cos.shape),
            whole(cos.shape),
            whole(cos.shape),
        ],
        out_specs=[strip(width), strip(q_cols), strip(kv_cols)],
        out_shape=[
            jax.ShapeDtypeStruct((rows, width), LOW),
            jax.ShapeDtypeStruct((rows, q_cols), LOW),
            jax.ShapeDtypeStruct((rows, kv_cols), LOW),
        ],
        compiler_params=pltpu.CompilerParams(vmem_limit_bytes=VMEM_LIMIT),
        cost_estimate=pl.CostEstimate(
            flops=2 * rows * width * padded,
            bytes_accessed=4 * rows * width + 2 * width * padded,
            transcendentals=0,
        ),
        name="project",
    )(flat, gain, weight, cos, ahead, behind)


def feed_kernel(input_ref, grad_ref, gate_ref, up_ref, down_ref, act_ref, grad_gate_ref, grad_up_ref):
    gate = dot(input_ref[...], gate_ref[...], 1, 0)
    up = dot(input_ref[...], up_ref[...], 1, 0)
    grad_act = dot(grad_ref[...], down_ref[...], 1, 0)
    sigmoid = jax.nn.sigmoid(gate)
    silu = gate * sigmoid
    act_ref[...] = (silu * up).astype(LOW)
    grad_gate_ref[...] = (grad_act * up * sigmoid * (1.0 + gate * (1.0 - sigmoid))).astype(LOW)
    grad_up_ref[...] = (grad_act * silu).astype(LOW)


def feed(inputs, grads, gate, up, down):
    rows, width = inputs.shape
    units = gate.shape[1]
    tile = 256
    whole = pl.BlockSpec((rows, width), lambda i: (0, 0))
    weight = pl.BlockSpec((width, tile), lambda i: (0, i))
    out = pl.BlockSpec((rows, tile), lambda i: (0, i))
    return pl.pallas_call(
        feed_kernel,
        grid=((units + tile - 1) // tile,),
        in_specs=[whole, whole, weight, weight, weight],
        out_specs=[out, out, out],
        out_shape=[jax.ShapeDtypeStruct((rows, units), LOW)] * 3,
        compiler_params=pltpu.CompilerParams(vmem_limit_bytes=VMEM_LIMIT),
        cost_estimate=pl.CostEstimate(
            flops=6 * rows * width * units // COST,
            bytes_accessed=(6 * width * units + 4 * rows * width + 6 * rows * units) // COST,
            transcendentals=0,
        ),
        name="feed",
    )(inputs, grads, gate, up, down)


def back_kernel(*refs):
    out_ref = refs[-1]
    count = (len(refs) - 1) // 2
    total = dot(refs[0][...], refs[count][...], 1, 1)
    for at in range(1, count):
        total += dot(refs[at][...], refs[count + at][...], 1, 1)
    out_ref[...] = total.astype(LOW)


def back_through(values, weights):
    rows, units = values[0].shape
    width = weights[0].shape[0]
    tile = 512
    count = len(values)
    return pl.pallas_call(
        back_kernel,
        grid=((width + tile - 1) // tile,),
        in_specs=[pl.BlockSpec((rows, units), lambda i: (0, 0))] * count
        + [pl.BlockSpec((tile, units), lambda i: (i, 0))] * count,
        out_specs=pl.BlockSpec((rows, tile), lambda i: (0, i)),
        out_shape=jax.ShapeDtypeStruct((rows, width), LOW),
        compiler_params=pltpu.CompilerParams(vmem_limit_bytes=VMEM_LIMIT),
        cost_estimate=pl.CostEstimate(
            flops=2 * count * rows * width * units // COST,
            bytes_accessed=(2 * count * (width + rows) * units + 2 * rows * width) // COST,
            transcendentals=0,
        ),
        name="back_through",
    )(*values, *weights)


def join_kernel(query_ref, kept_ref, landed_ref, cos_ref, ahead_ref, behind_ref, out_ref):
    q_cols, kv_cols = query_ref.shape[1], kept_ref.shape[1]
    local, padded = cos_ref.shape
    out_ref[:, :q_cols] = query_ref[...]
    for start in range(0, kept_ref.shape[0], local):
        rows = slice(start, start + local)
        part = kept_ref[rows, :].astype(jnp.float32) + landed_ref[rows, :].astype(jnp.float32)
        if padded > kv_cols:
            part = jnp.concatenate(
                [part, jnp.zeros((local, padded - kv_cols), jnp.float32)], axis=1
            )
        turned = (
            part * cos_ref[...]
            - pltpu.roll(part, padded - HD // 2, 1) * ahead_ref[...]
            - pltpu.roll(part, HD // 2, 1) * behind_ref[...]
        ).astype(LOW)
        out_ref[rows, q_cols : q_cols + kv_cols] = turned[:, :kv_cols]


def join_back(query, kept, landed, cos, ahead, behind):
    rows, q_cols = query.shape
    return pl.pallas_call(
        join_kernel,
        out_shape=jax.ShapeDtypeStruct((rows, q_cols + kept.shape[1]), LOW),
        compiler_params=pltpu.CompilerParams(vmem_limit_bytes=VMEM_LIMIT),
        cost_estimate=pl.CostEstimate(flops=0, bytes_accessed=8 * kept.size, transcendentals=0),
        name="join_back",
    )(query, kept, landed, cos, ahead, behind)


def stack_heads(block, group, per):
    return jnp.concatenate(
        [block[:, (group * per + h) * HD : (group * per + h + 1) * HD] for h in range(per)],
        axis=0,
    )


def key_block(own_ref, other_ref, at, column):
    return jnp.concatenate(
        [own_ref[at, :, column : column + HD], other_ref[at, :, column : column + HD]],
        axis=0,
    )


def key_limits(meta_ref, slots_ref, local):
    me, length = meta_ref[0], meta_ref[1 + pl.program_id(0)]
    pair = 2 * local
    full = lax.div(jnp.minimum(me * local + 1, length), pair)
    some = lax.div(jnp.minimum((me + 1) * local, length) + pair - 1, pair)
    limit = jnp.minimum(slots_ref[...], length - 1)
    row = lax.broadcasted_iota(jnp.int32, (pair, 1), 0)
    core = lax.rem(me, 2)
    within = jnp.where(row < local, core * local + row, (1 - core) * local + row - local)
    return me, length, full, some, limit, within


def keep_allowed(scores, base, within, limit, slots, window):
    place = base + within
    allowed = place <= limit
    if window:
        allowed = allowed & (slots - place < WINDOW)
    return jnp.where(allowed, scores, NEGATIVE)


def attend_kernel(meta_ref, slots_ref, query_ref, own_ref, other_ref, att_ref, lse_ref, stacked, total, *, groups, per, window):
    local = query_ref.shape[0]
    pair = 2 * local
    kv_cols = groups * HD
    me, _, full, some, limit, within = key_limits(meta_ref, slots_ref, local)
    if window:
        full = full * 0
    factor = HD ** (-0.5) * LOG2E
    for g in range(groups):
        stacked[g] = stack_heads(query_ref[...], g, per)
        total[g] = jnp.zeros(total.shape[1:], jnp.float32)

    def step(m, carry, masked):
        at = jnp.bitwise_xor(m, lax.div(me, 2))
        out = []
        for g in range(groups):
            top, weight = carry[g]
            keys = key_block(own_ref, other_ref, at, g * HD)
            values = key_block(own_ref, other_ref, at, kv_cols + g * HD)
            scores = dot(keys, stacked[g], 1, 1) * factor
            if masked:
                scores = keep_allowed(scores, m * pair, within, limit, slots_ref[...], window)
            higher = jnp.maximum(top, jnp.max(scores, axis=0, keepdims=True))
            probs = jnp.exp2(scores - higher)
            shrink = jnp.exp2(top - higher)
            total[g] = total[g] * shrink + dot(values, probs.astype(LOW), 0, 0)
            out.append(
                (higher, weight * shrink + jnp.sum(probs, axis=0, keepdims=True))
            )
        return tuple(out)

    row = (1, per * local)
    carry = tuple(
        (jnp.full(row, NEGATIVE, jnp.float32), jnp.zeros(row, jnp.float32))
        for _ in range(groups)
    )
    carry = lax.fori_loop(0, full, lambda m, c: step(m, c, False), carry)
    carry = lax.fori_loop(full, some, lambda m, c: step(m, c, True), carry)
    for g in range(groups):
        top, weight = carry[g]
        lse_ref[0, g : g + 1, :] = top + jnp.log2(weight)
        out = (total[g] / weight).T.astype(LOW)
        for h in range(per):
            at = (g * per + h) * HD
            att_ref[:, at : at + HD] = out[h * local : (h + 1) * local]


def attend_back_kernel(
    meta_ref, slots_ref, cos_ref, sin_ref, query_ref, own_ref, other_ref, att_ref, grad_ref, lse_ref,
    grad_query_ref, grad_own_ref, grad_other_ref, stacked, stacked_grad, total, row_dot, *, groups, per, window,
):
    local = query_ref.shape[0]
    pair = 2 * local
    kv_cols = groups * HD
    me, length, full, some, limit, within = key_limits(meta_ref, slots_ref, local)
    if window:
        full = full * 0
    scale = HD ** (-0.5)
    live = me * local < length
    full = jnp.where(live, full, 0)
    some = jnp.where(live, some, 0)
    chips = own_ref.shape[0]
    chip = lax.div(me, 2)

    for g in range(groups):
        stacked[g] = stack_heads(query_ref[...], g, per)
        grads = stack_heads(grad_ref[...], g, per)
        stacked_grad[g] = grads
        product = grads.astype(jnp.float32) * stack_heads(att_ref[...], g, per).astype(jnp.float32)
        row_dot[g : g + 1, :] = jnp.sum(product.T, axis=0, keepdims=True)
        total[g] = jnp.zeros(total.shape[1:], jnp.float32)

    def clear(m, carry):
        at = jnp.bitwise_xor(m, chip)
        grad_own_ref[at] = jnp.zeros(grad_own_ref.shape[1:], LOW)
        grad_other_ref[at] = jnp.zeros(grad_other_ref.shape[1:], LOW)
        return carry

    def step(m, carry, masked):
        at = jnp.bitwise_xor(m, chip)
        for g in range(groups):
            keys = key_block(own_ref, other_ref, at, g * HD)
            values = key_block(own_ref, other_ref, at, kv_cols + g * HD)
            scores = dot(keys, stacked[g], 1, 1) * (scale * LOG2E)
            if masked:
                scores = keep_allowed(scores, m * pair, within, limit, slots_ref[...], window)
            probs = jnp.exp2(scores - lse_ref[0, g : g + 1, :])
            grad_probs = dot(values, stacked_grad[g], 1, 1)
            grad_scores = (probs * (grad_probs - row_dot[g : g + 1, :])).astype(LOW)
            grad_values = dot(probs.astype(LOW), stacked_grad[g], 1, 0).astype(LOW)
            grad_keys = (dot(grad_scores, stacked[g], 1, 0) * scale).astype(LOW)
            total[g] += dot(keys, grad_scores, 0, 0)
            for column, grads in ((g * HD, grad_keys), (kv_cols + g * HD, grad_values)):
                grad_own_ref[at, :, column : column + HD] = grads[:local]
                grad_other_ref[at, :, column : column + HD] = grads[local:]
        return carry

    lax.fori_loop(0, full, lambda m, c: step(m, c, False), 0)
    lax.fori_loop(full, some, lambda m, c: step(m, c, True), 0)
    lax.fori_loop(some, chips, clear, 0)
    half = HD // 2
    cos, sin = cos_ref[...], sin_ref[...]
    for g in range(groups):
        grads = total[g] * scale
        first, second = grads[:half], grads[half:]
        turned = jnp.concatenate(
            [first * cos + second * sin, second * cos - first * sin], axis=0
        ).T.astype(LOW)
        for h in range(per):
            at = (g * per + h) * HD
            grad_query_ref[:, at : at + HD] = turned[h * local : (h + 1) * local]


def attention_specs(seqs, local, q_cols, kv_both, chips, groups, columns):
    meta = pl.BlockSpec(memory_space=pltpu.SMEM)
    whole = lambda shape: pl.BlockSpec(shape, lambda s: (0,) * len(shape))
    queries = pl.BlockSpec((local, q_cols), lambda s: (s, 0))
    keys = pl.BlockSpec((chips, local, kv_both), lambda s: (0, s, 0))
    lse = pl.BlockSpec((1, groups, columns), lambda s: (s, 0, 0))
    return meta, whole, queries, keys, lse


def attend(meta, slots, query, own, other, groups, window):
    seqs = meta.shape[0] - 1
    rows, q_cols = query.shape
    local = rows // seqs
    chips, _, kv_both = own.shape
    per = q_cols // HD // groups
    columns = per * local
    smem, whole, queries, keys, lse = attention_specs(
        seqs, local, q_cols, kv_both, chips, groups, columns
    )
    pairs = rows * q_cols // HD * 2 * chips * local
    return pl.pallas_call(
        functools.partial(attend_kernel, groups=groups, per=per, window=window),
        grid=(seqs,),
        in_specs=[smem, whole((1, columns)), queries, keys, keys],
        out_specs=[queries, lse],
        out_shape=[
            jax.ShapeDtypeStruct((rows, q_cols), LOW),
            jax.ShapeDtypeStruct((seqs, groups, columns), jnp.float32),
        ],
        scratch_shapes=[
            pltpu.VMEM((groups, columns, HD), LOW),
            pltpu.VMEM((groups, HD, columns), jnp.float32),
        ],
        compiler_params=pltpu.CompilerParams(vmem_limit_bytes=VMEM_LIMIT),
        cost_estimate=pl.CostEstimate(
            flops=12 * pairs * HD // COST, bytes_accessed=4 * own.size // COST, transcendentals=0
        ),
        name="attend",
    )(meta, slots, query, own, other)


def attend_back(meta, slots, cos, sin, query, own, other, att, grad, lse_rows, groups, window):
    seqs = meta.shape[0] - 1
    rows, q_cols = query.shape
    local = rows // seqs
    chips, _, kv_both = own.shape
    per = q_cols // HD // groups
    columns = per * local
    smem, whole, queries, keys, lse = attention_specs(
        seqs, local, q_cols, kv_both, chips, groups, columns
    )
    pairs = rows * q_cols // HD * 2 * chips * local
    return pl.pallas_call(
        functools.partial(attend_back_kernel, groups=groups, per=per, window=window),
        grid=(seqs,),
        in_specs=[
            smem, whole((1, columns)), whole(cos.shape), whole(cos.shape),
            queries, keys, keys, queries, queries, lse,
        ],
        out_specs=[queries, keys, keys],
        out_shape=[
            jax.ShapeDtypeStruct((rows, q_cols), LOW),
            jax.ShapeDtypeStruct(own.shape, LOW),
            jax.ShapeDtypeStruct(own.shape, LOW),
        ],
        scratch_shapes=[
            pltpu.VMEM((groups, columns, HD), LOW),
            pltpu.VMEM((groups, columns, HD), LOW),
            pltpu.VMEM((groups, HD, columns), jnp.float32),
            pltpu.VMEM((groups, columns), jnp.float32),
        ],
        compiler_params=pltpu.CompilerParams(vmem_limit_bytes=VMEM_LIMIT),
        cost_estimate=pl.CostEstimate(
            flops=30 * pairs * HD // COST, bytes_accessed=8 * own.size // COST, transcendentals=0
        ),
        name="attend_back",
    )(meta, slots, cos, sin, query, own, other, att, grad, lse_rows)


def take_chunk(rows, index, size):
    return lax.dynamic_slice_in_dim(rows, index * size, size, axis=0)


def norm_scale(values):
    return lax.rsqrt(jnp.mean(values * values, axis=-1, keepdims=True) + EPSILON)


def norm_back(grad, gain, normed, scale):
    scaled = grad * gain
    return scale * (scaled - normed * jnp.mean(scaled * normed, axis=-1, keepdims=True))


def per_device(
    tokens,
    lengths,
    cotangent,
    attn_gain,
    query_weight,
    key_weight,
    value_weight,
    out_weight,
    ffn_gain,
    gate_weight,
    up_weight,
    down_weight,
):
    micro_count, seq_count, local_tokens, width = tokens.shape
    place = line_place(lax.axis_index("head"))
    me = lax.axis_index("ctx")
    lines = lax.axis_size("head")
    q_cols = query_weight.shape[1]
    kv_cols = key_weight.shape[1]
    used = q_cols + 2 * kv_cols
    padded = (used + 2 + 127) // 128 * 128

    qkv_shard = jnp.concatenate(
        [
            query_weight,
            key_weight,
            value_weight,
            attn_gain[:, None],
            ffn_gain[:, None],
            jnp.zeros((query_weight.shape[0], padded - used - 2), LOW),
        ],
        axis=1,
    )
    full_qkv = lax.all_gather(qkv_shard, "ctx", axis=0, tiled=True)
    full_out = lax.all_gather(out_weight.T, "ctx", axis=0, tiled=True)
    full_gate = lax.all_gather(gate_weight, "ctx", axis=0, tiled=True)
    full_up = lax.all_gather(up_weight, "ctx", axis=0, tiled=True)
    full_down = lax.all_gather(down_weight.T, "ctx", axis=0, tiled=True)
    gains = full_qkv[:, used : used + 2].T.astype(jnp.float32)
    gain_attn = gains[0:1]
    gain_ffn = gains[1:2]

    heads = q_cols // HD
    groups = kv_cols // HD
    per = heads // groups
    span_total = local_tokens * lax.axis_size("ctx")
    window = span_total > WINDOW
    query_slots = me * local_tokens + jnp.arange(local_tokens, dtype=jnp.int32)
    cosine, sine = angles(query_slots)
    piece_rows = seq_count * local_tokens
    rows = micro_count * piece_rows
    chunk = piece_rows // lines
    pieces = range(micro_count)

    nothing = jnp.zeros_like(sine)
    turning = heads + groups
    rest = padded - turning * HD
    cos_wide = jnp.concatenate(
        [cosine] * (2 * turning) + [jnp.ones((local_tokens, rest), jnp.float32)], axis=1
    )
    ahead = jnp.concatenate(
        [-sine, nothing] * turning + [jnp.zeros((local_tokens, rest), jnp.float32)], axis=1
    )
    behind = jnp.concatenate(
        [nothing, sine] * turning + [jnp.zeros((local_tokens, rest), jnp.float32)], axis=1
    )
    both = 2 * kv_cols
    rest = (both + 127) // 128 * 128 - groups * HD
    key_tables = (
        jnp.concatenate(
            [cosine] * (2 * groups) + [jnp.ones((local_tokens, rest), jnp.float32)], axis=1
        ),
        jnp.concatenate(
            [-sine, nothing] * groups + [jnp.zeros((local_tokens, rest), jnp.float32)], axis=1
        ),
        jnp.concatenate(
            [nothing, sine] * groups + [jnp.zeros((local_tokens, rest), jnp.float32)], axis=1
        ),
    )
    cos_tall = jnp.concatenate([cosine.T] * per, axis=1)
    sin_tall = jnp.concatenate([sine.T] * per, axis=1)
    slots = jnp.concatenate([query_slots] * per)[None]

    flat = tokens.reshape(rows, width)
    input_one, query_rot, kv = project(
        flat, gain_attn, full_qkv, cos_wide, ahead, behind, micro_count, q_cols, 2 * kv_cols
    )

    def piece_of(array, piece):
        return array[piece * piece_rows : (piece + 1) * piece_rows]

    live = (query_slots[None, None, :] < lengths[:, :, None]).reshape(rows, 1)
    grad_out = jnp.where(live, cotangent.reshape(rows, width), 0)

    metas = [
        jnp.concatenate([me.astype(jnp.int32)[None], lengths[piece]]) for piece in pieces
    ]
    bits = chip_bits()
    keys = [
        cube_gather(piece_of(kv, piece), bits if piece % 2 == 0 else bits[::-1])
        for piece in pieces
    ]

    def attend_piece(piece, *others):
        own, other = keys[piece]
        query = after(piece_of(query_rot, piece), *others)
        att, lse = attend(metas[piece], slots, query, own, other, groups, window)
        return att, lse, dot(att, full_out, 1, 1).astype(LOW)

    def residual(piece, summed):
        piece_tokens = take_chunk(piece_of(flat, piece), place, chunk).astype(jnp.float32)
        hidden = piece_tokens + summed
        scale = norm_scale(hidden)
        normed = hidden * scale
        return hidden, scale, normed, (normed * gain_ffn).astype(LOW)

    def hidden_back(piece, grad_two, kept):
        _, scale, normed, _ = kept
        gain_term = jnp.sum(grad_two * normed, axis=0)
        grad_hidden = take_chunk(piece_of(grad_out, piece), place, chunk).astype(
            jnp.float32
        ) + norm_back(grad_two, gain_ffn, normed, scale)
        return gain_term, grad_hidden, grad_hidden.astype(LOW)

    def scatter_weight(term):
        return lax.psum_scatter(term, "ctx", scatter_dimension=0, tiled=True)

    def weight_grad(left, right, *others):
        term = dot(after(left, *others), right, 0, 0).astype(LOW)
        return with_layout_constraint(term, Layout((0, 1)))

    def attention_back(piece, grad_low, *others):
        grad_att = dot(after(grad_low, *others), full_out, 1, 0).astype(LOW)
        own, other = keys[piece]
        return attend_back(
            metas[piece], slots, cos_tall, sin_tall, piece_of(query_rot, piece), own, other,
            atts[piece], grad_att, lses[piece], groups, window,
        )

    def one_back(back, *others):
        return dot(after(back, *others), full_qkv[:, :used], 1, 1).astype(LOW)

    def tokens_back(piece, grad_one, grad_hidden):
        piece_tokens = take_chunk(piece_of(flat, piece), place, chunk).astype(jnp.float32)
        scale = norm_scale(piece_tokens)
        normed = piece_tokens * scale
        gain_term = jnp.sum(grad_one * normed, axis=0)
        total = grad_hidden + norm_back(grad_one, gain_attn, normed, scale)
        return gain_term, total.astype(LOW)

    att0, lse0, branch0 = attend_piece(0)
    sum0 = ChainScatter(branch0)
    sum0.next()
    att1, lse1, branch1 = attend_piece(1, branch0)
    atts, lses = (att0, att1), (lse0, lse1)
    sum1 = ChainScatter(branch1, *sum0.landed)
    kept0 = residual(0, sum0.finish())
    two0 = ChainGather(kept0[3])
    sum1.next()
    two0.next()
    two0.next(full_gate, full_up)
    kept1 = residual(1, sum1.finish())
    two1 = Gather(kept1[3])
    input0 = two0.finish()

    act0, grad_gate0, grad_up0 = feed(
        after(input0, kept1[3]), piece_of(grad_out, 0), full_gate, full_up, full_down
    )
    two1.next(full_down)
    back_two0 = back_through((after(grad_gate0, two1.landed), grad_up0), (full_gate, full_up))
    back_sum0 = Scatter(back_two0)
    input1 = two1.finish()
    act1, grad_gate1, grad_up1 = feed(
        after(input1, back_two0), piece_of(grad_out, 1), full_gate, full_up, full_down
    )
    back_sum0.next(act1)
    acts = jnp.concatenate([act0, act1], axis=0)
    down_term = weight_grad(grad_out, acts, back_sum0.kept)
    down_grad = scatter_weight(down_term)
    back_two1 = back_through((after(grad_gate1, down_term), grad_up1), (full_gate, full_up))
    gain0, grad_hidden0, low0 = hidden_back(0, back_sum0.finish(back_two1), kept0)
    hidden0 = Gather(low0)
    back_sum1 = Scatter(back_two1)
    ffn = back_through((after(acts, low0, back_two1),), (full_down,))
    input_two = jnp.concatenate([input0, input1], axis=0)
    gate_term = weight_grad(
        input_two,
        jnp.concatenate([grad_gate0, grad_gate1], axis=0),
        ffn,
        back_sum1.landed,
        hidden0.landed,
    )
    gate_grad = scatter_weight(gate_term)
    hidden0.next()
    back_sum1.next()
    up_term = weight_grad(
        input_two, jnp.concatenate([grad_up0, grad_up1], axis=0), gate_term
    )
    up_grad = scatter_weight(up_term)
    whole0 = hidden0.finish(up_term)
    mixed0 = Scatter(piece_of(ffn, 0), whole0)
    gain1, grad_hidden1, low1 = hidden_back(1, back_sum1.finish(up_term), kept1)
    hidden1 = Gather(low1)
    query0, own0, other0 = attention_back(0, whole0, low1)
    keys0 = Reduce(own0, other0, bits)
    hidden1.next()
    keys0.next(mixed0.landed)
    mixed0.next()
    whole1 = hidden1.finish()
    mixed1 = Scatter(piece_of(ffn, 1), whole1)
    whole_mixed0 = Gather((kept0[0] + mixed0.finish()).astype(LOW))
    query1, own1, other1 = attention_back(
        1, whole1, query0, keys0.sent, mixed1.held
    )
    keys1 = Reduce(own1, other1, bits)
    keys0.next(mixed1.landed)
    mixed1.next()
    whole_mixed0.next()
    keys1.next()
    back0 = join_back(query0, *keys0.finish(), *key_tables)
    back_one0 = one_back(back0, query1, keys1.sent)
    one0 = Scatter(back_one0)
    whole_mixed1 = Gather((kept1[0] + mixed1.finish()).astype(LOW))
    keys1.next()
    back1 = join_back(query1, *keys1.finish(), *key_tables)
    back_one1 = one_back(back1, back_one0, one0.held)
    one1 = Scatter(back_one1)
    one0.next()
    whole_mixed1.next()
    last_term = jnp.concatenate(
        [
            weight_grad(
                input_one, jnp.concatenate([back0, back1], axis=0), back_one1, gate_grad
            ),
            weight_grad(
                jnp.concatenate([whole0, whole1], axis=0),
                jnp.concatenate([att0, att1], axis=0),
                back_one1,
            ),
        ],
        axis=1,
    )
    last_grad = scatter_weight(last_term).astype(jnp.float32)
    qkv_grad, out_grad = last_grad[:, :used], last_grad[:, used:]
    gain2, total0 = tokens_back(0, one0.finish(), grad_hidden0)
    tokens0 = ChainGather(total0)
    tokens0_first = tokens0.landed
    one1.next()
    tokens0.next()
    gain3, total1 = tokens_back(1, one1.finish(tokens0_first), grad_hidden1)
    tokens1 = ChainGather(total1)
    gain_terms = after(jnp.stack([gain2 + gain3, gain0 + gain1]), total1)
    for bit in line_bits():
        gain_terms = gain_terms + line_swap(gain_terms, bit)
    gain_terms = jnp.swapaxes(
        gain_terms.reshape(2, lax.axis_size("ctx"), attn_gain.shape[0]), 0, 1
    )
    for bit in (bits[::-1] + [1]):
        half = gain_terms.shape[0] // 2
        mine = lax.rem(me // bit, 2)
        got = lax.ppermute(take_chunk(gain_terms, 1 - mine, half), "ctx", flip(bit))
        gain_terms = take_chunk(gain_terms, mine, half) + got
    gain_terms = gain_terms[0]
    gate_out = gate_grad.astype(jnp.float32)
    up_out = up_grad.astype(jnp.float32)
    down_out = down_grad.T.astype(jnp.float32)
    tokens1.next(gain_terms)
    mixed = jnp.stack([whole_mixed0.finish(), whole_mixed1.finish()], axis=0).reshape(tokens.shape)
    token_grad = (
        jnp.stack([tokens0.finish(), tokens1.finish(gate_out, up_out, down_out)], axis=0)
        .reshape(tokens.shape)
        .astype(jnp.float32)
    )
    return (
        mixed,
        token_grad,
        gain_terms[0],
        qkv_grad[:, :q_cols],
        qkv_grad[:, q_cols : q_cols + kv_cols],
        qkv_grad[:, q_cols + kv_cols :],
        out_grad.T,
        gain_terms[1],
        gate_out,
        up_out,
        down_out,
    )


def solution(mesh):
    placed = (
        P(None, None, "ctx", None),
        P(),
        P(None, None, "ctx", None),
        P("ctx"),
        P("ctx", "head"),
        P("ctx", "head"),
        P("ctx", "head"),
        P("head", "ctx"),
        P("ctx"),
        P("ctx", "head"),
        P("ctx", "head"),
        P("head", "ctx"),
    )
    return jax.shard_map(
        per_device,
        mesh=mesh,
        in_specs=placed,
        out_specs=(
            P(None, None, "ctx", None),
            P(None, None, "ctx", None),
            P("ctx"),
            P("ctx", "head"),
            P("ctx", "head"),
            P("ctx", "head"),
            P("head", "ctx"),
            P("ctx"),
            P("ctx", "head"),
            P("ctx", "head"),
            P("head", "ctx"),
        ),
        check_vma=False,
    )
```

```python
import functools

import jax
import jax.numpy as jnp
from jax import lax
from jax.experimental.layout import Layout, with_layout_constraint
from jax.experimental import pallas as pl
from jax.experimental.pallas import tpu as pltpu
from jax.sharding import PartitionSpec as P

HD = 80
WINDOW = 4096

EPSILON = 1e-05
THETA_BASE = 10000.0
NEGATIVE = -1e30
LOG2E = 1.4426950408889634
LOW = jnp.bfloat16
VMEM_LIMIT = 48 * 1024 * 1024
COST = 2


def dot(left, right, a, b):
    return lax.dot_general(
        left, right, (((a,), (b,)), ((), ())), preferred_element_type=jnp.float32
    )


def after(value, *others):
    if not others:
        return value
    return lax.optimization_barrier((value, others))[0]


def angles(positions):
    half = HD // 2
    freq = THETA_BASE ** (-jnp.arange(half, dtype=jnp.float32) * 2.0 / HD)
    angle = positions.astype(jnp.float32)[:, None] * freq[None, :]
    return jnp.cos(angle), jnp.sin(angle)


def add_low(*terms):
    return sum(term.astype(jnp.float32) for term in terms).astype(LOW)


def flip(bit):
    n = lax.axis_size("ctx")
    return [(i, i ^ bit) for i in range(n)]


def chip_bits():
    bits, bit = [], 2
    while bit < lax.axis_size("ctx"):
        bits.append(bit)
        bit *= 2
    return bits


def cube_gather(part, bits):
    own, places = part[None], [0]
    for bit in bits:
        got = lax.ppermute(own, "ctx", flip(bit))
        own = jnp.concatenate([own, got], axis=0)
        places = places + [place ^ (bit // 2) for place in places]
    order = [places.index(m) for m in range(len(places))]
    if order != sorted(order):
        own = jnp.stack([own[at] for at in order], axis=0)
    return own, lax.ppermute(own, "ctx", flip(1))


def line_bits():
    bits, bit = [], 1
    while bit < lax.axis_size("head"):
        bits.append(bit)
        bit *= 2
    return bits


def line_swap(value, bit):
    n = lax.axis_size("head")
    return lax.ppermute(value, "head", [(i, i ^ bit) for i in range(n)])


def line_place(z):
    place = z * 0
    for bit in line_bits():
        place = place * 2 + lax.rem(z // bit, 2)
    return place


class Scatter:
    def __init__(self, partial, *others):
        self.held = after(partial, *others)
        self.bits = line_bits()
        self.send()

    def send(self):
        half = self.held.shape[0] // 2
        mine = lax.rem(lax.axis_index("head") // self.bits[0], 2)
        self.landed = line_swap(
            take_chunk(self.held, 1 - mine, half).astype(LOW), self.bits[0]
        )
        self.kept = take_chunk(self.held, mine, half).astype(jnp.float32)
        self.bits = self.bits[1:]

    def land(self):
        self.held = self.kept + self.landed.astype(jnp.float32)

    def next(self, *others):
        self.landed = after(self.landed, *others)
        self.land()
        self.send()
        return self

    def finish(self, *others):
        while self.bits:
            self.next()
        self.landed = after(self.landed, *others)
        self.land()
        return self.held


class Gather:
    def __init__(self, chunk, *others):
        self.held = after(chunk, *others)
        self.bits = line_bits()[::-1]
        self.send()

    def send(self):
        self.mine = lax.rem(lax.axis_index("head") // self.bits[0], 2)
        self.landed = line_swap(self.held, self.bits[0])
        self.bits = self.bits[1:]

    def land(self):
        first = jnp.where(self.mine == 0, self.held, self.landed)
        second = jnp.where(self.mine == 0, self.landed, self.held)
        self.held = jnp.concatenate([first, second], axis=0)

    def next(self, *others):
        self.landed = after(self.landed, *others)
        self.land()
        self.send()
        return self

    def finish(self, *others):
        while self.bits:
            self.next()
        self.landed = after(self.landed, *others)
        self.land()
        return self.held


class ChainScatter:
    def __init__(self, partial, *others):
        self.partial = self.held = after(partial, *others)
        self.step = 0
        self.send()

    def block(self, z):
        n = lax.axis_size("head")
        size = self.partial.shape[0] // n
        return take_chunk(self.partial, line_place(jnp.clip(z, 0, n - 1)), size)

    def send(self):
        n = lax.axis_size("head")
        z = lax.axis_index("head")
        step = self.step
        rising = self.block(n - 1 - step + z)
        falling = self.block(step + z - (n - 1))
        if step:
            rising = add_low(rising, self.landed[0])
            falling = add_low(falling, self.landed[1])
        self.landed = (
            lax.ppermute(rising, "head", [(i, i + 1) for i in range(step + 1)]),
            lax.ppermute(falling, "head", [(i, i - 1) for i in range(n - 1 - step, n)]),
        )
        self.step += 1

    def next(self, *others):
        self.landed = (after(self.landed[0], *others), self.landed[1])
        self.send()
        return self

    def finish(self, *others):
        while self.step < lax.axis_size("head") - 1:
            self.next()
        mine = after(self.block(lax.axis_index("head")), *others)
        return sum(part.astype(jnp.float32) for part in (mine,) + self.landed)


class ChainGather:
    def __init__(self, chunk, *others):
        self.chunk = after(chunk, *others)
        self.landed = (self.chunk, self.chunk)
        self.got = []
        self.send()

    def send(self):
        n = lax.axis_size("head")
        step = len(self.got)
        self.landed = (
            lax.ppermute(self.landed[0], "head", [(i, i + 1) for i in range(step, n - 1)]),
            lax.ppermute(self.landed[1], "head", [(i, i - 1) for i in range(1, n - step)]),
        )
        self.got.append(self.landed)

    def next(self, *others):
        self.landed = (after(self.landed[0], *others), self.landed[1])
        self.send()
        return self

    def finish(self, *others):
        n = lax.axis_size("head")
        z = lax.axis_index("head")
        while len(self.got) < n - 1:
            self.next()
        size = self.chunk.shape[0]
        whole = jnp.zeros((n * size,) + self.chunk.shape[1:], self.chunk.dtype)
        whole = lax.dynamic_update_slice_in_dim(
            whole, after(self.chunk, *others), line_place(z) * size, axis=0
        )
        for step in range(n - 1):
            block = jnp.where(z > step, self.got[step][0], self.got[n - 2 - step][1])
            at = line_place(lax.rem(z - 1 - step + n, n)) * size
            whole = lax.dynamic_update_slice_in_dim(whole, block, at, axis=0)
        return whole


class Reduce:
    def __init__(self, own, other, bits):
        self.bits = bits[::-1]
        self.kept = own
        self.landed = lax.ppermute(other, "ctx", flip(1))

    def next(self, *others):
        landed = after(self.landed, *others)
        bit, self.bits = self.bits[0], self.bits[1:]
        half = self.kept.shape[0] // 2
        sent = add_low(self.kept[half:], landed[half:])
        self.kept = add_low(self.kept[:half], landed[:half])
        self.sent = sent
        self.landed = lax.ppermute(sent, "ctx", flip(bit))

    def finish(self):
        while self.bits:
            self.next()
        return self.kept[0], self.landed[0]


def project_kernel(tokens_ref, gain_ref, weight_ref, cos_ref, ahead_ref, behind_ref, normed_ref, query_ref, kv_ref):
    values = tokens_ref[...].astype(jnp.float32)
    scale = lax.rsqrt(jnp.mean(values * values, axis=-1, keepdims=True) + EPSILON)
    normed = (values * scale * gain_ref[...]).astype(LOW)
    normed_ref[...] = normed
    out = dot(normed, weight_ref[...], 1, 0)
    local, padded = cos_ref.shape
    q_cols, kv_cols = query_ref.shape[1], kv_ref.shape[1]
    for start in range(0, out.shape[0], local):
        part = out[start : start + local]
        turned = (
            part * cos_ref[...]
            + pltpu.roll(part, padded - HD // 2, 1) * ahead_ref[...]
            + pltpu.roll(part, HD // 2, 1) * behind_ref[...]
        ).astype(LOW)
        query_ref[start : start + local, :] = turned[:, :q_cols]
        kv_ref[start : start + local, :] = turned[:, q_cols : q_cols + kv_cols]


def project(flat, gain, weight, cos, ahead, behind, pieces, q_cols, kv_cols):
    rows, width = flat.shape
    size = rows // pieces
    padded = weight.shape[1]
    whole = lambda shape: pl.BlockSpec(shape, lambda i: (0,) * len(shape))
    strip = lambda columns: pl.BlockSpec((size, columns), lambda i: (i, 0))
    return pl.pallas_call(
        project_kernel,
        grid=(pieces,),
        in_specs=[
            strip(width),
            whole((1, width)),
            whole((width, padded)),
            whole(cos.shape),
            whole(cos.shape),
            whole(cos.shape),
        ],
        out_specs=[strip(width), strip(q_cols), strip(kv_cols)],
        out_shape=[
            jax.ShapeDtypeStruct((rows, width), LOW),
            jax.ShapeDtypeStruct((rows, q_cols), LOW),
            jax.ShapeDtypeStruct((rows, kv_cols), LOW),
        ],
        compiler_params=pltpu.CompilerParams(vmem_limit_bytes=VMEM_LIMIT),
        cost_estimate=pl.CostEstimate(
            flops=2 * rows * width * padded,
            bytes_accessed=4 * rows * width + 2 * width * padded,
            transcendentals=0,
        ),
        name="project",
    )(flat, gain, weight, cos, ahead, behind)


def feed_kernel(input_ref, grad_ref, gate_ref, up_ref, down_ref, act_ref, grad_gate_ref, grad_up_ref):
    gate = dot(input_ref[...], gate_ref[...], 1, 0)
    up = dot(input_ref[...], up_ref[...], 1, 0)
    grad_act = dot(grad_ref[...], down_ref[...], 1, 0)
    sigmoid = jax.nn.sigmoid(gate)
    silu = gate * sigmoid
    act_ref[...] = (silu * up).astype(LOW)
    grad_gate_ref[...] = (grad_act * up * sigmoid * (1.0 + gate * (1.0 - sigmoid))).astype(LOW)
    grad_up_ref[...] = (grad_act * silu).astype(LOW)


def feed(inputs, grads, gate, up, down):
    rows, width = inputs.shape
    units = gate.shape[1]
    tile = 256
    whole = pl.BlockSpec((rows, width), lambda i: (0, 0))
    weight = pl.BlockSpec((width, tile), lambda i: (0, i))
    out = pl.BlockSpec((rows, tile), lambda i: (0, i))
    return pl.pallas_call(
        feed_kernel,
        grid=((units + tile - 1) // tile,),
        in_specs=[whole, whole, weight, weight, weight],
        out_specs=[out, out, out],
        out_shape=[jax.ShapeDtypeStruct((rows, units), LOW)] * 3,
        compiler_params=pltpu.CompilerParams(vmem_limit_bytes=VMEM_LIMIT),
        cost_estimate=pl.CostEstimate(
            flops=6 * rows * width * units // COST,
            bytes_accessed=(6 * width * units + 4 * rows * width + 6 * rows * units) // COST,
            transcendentals=0,
        ),
        name="feed",
    )(inputs, grads, gate, up, down)


def back_kernel(*refs):
    out_ref = refs[-1]
    count = (len(refs) - 1) // 2
    total = dot(refs[0][...], refs[count][...], 1, 1)
    for at in range(1, count):
        total += dot(refs[at][...], refs[count + at][...], 1, 1)
    out_ref[...] = total.astype(LOW)


def back_through(values, weights):
    rows, units = values[0].shape
    width = weights[0].shape[0]
    tile = 512
    count = len(values)
    return pl.pallas_call(
        back_kernel,
        grid=((width + tile - 1) // tile,),
        in_specs=[pl.BlockSpec((rows, units), lambda i: (0, 0))] * count
        + [pl.BlockSpec((tile, units), lambda i: (i, 0))] * count,
        out_specs=pl.BlockSpec((rows, tile), lambda i: (0, i)),
        out_shape=jax.ShapeDtypeStruct((rows, width), LOW),
        compiler_params=pltpu.CompilerParams(vmem_limit_bytes=VMEM_LIMIT),
        cost_estimate=pl.CostEstimate(
            flops=2 * count * rows * width * units // COST,
            bytes_accessed=(2 * count * (width + rows) * units + 2 * rows * width) // COST,
            transcendentals=0,
        ),
        name="back_through",
    )(*values, *weights)


def join_kernel(query_ref, kept_ref, landed_ref, cos_ref, ahead_ref, behind_ref, out_ref):
    q_cols, kv_cols = query_ref.shape[1], kept_ref.shape[1]
    local, padded = cos_ref.shape
    out_ref[:, :q_cols] = query_ref[...]
    for start in range(0, kept_ref.shape[0], local):
        rows = slice(start, start + local)
        part = kept_ref[rows, :].astype(jnp.float32) + landed_ref[rows, :].astype(jnp.float32)
        if padded > kv_cols:
            part = jnp.concatenate(
                [part, jnp.zeros((local, padded - kv_cols), jnp.float32)], axis=1
            )
        turned = (
            part * cos_ref[...]
            - pltpu.roll(part, padded - HD // 2, 1) * ahead_ref[...]
            - pltpu.roll(part, HD // 2, 1) * behind_ref[...]
        ).astype(LOW)
        out_ref[rows, q_cols : q_cols + kv_cols] = turned[:, :kv_cols]


def join_back(query, kept, landed, cos, ahead, behind):
    rows, q_cols = query.shape
    return pl.pallas_call(
        join_kernel,
        out_shape=jax.ShapeDtypeStruct((rows, q_cols + kept.shape[1]), LOW),
        compiler_params=pltpu.CompilerParams(vmem_limit_bytes=VMEM_LIMIT),
        cost_estimate=pl.CostEstimate(flops=0, bytes_accessed=8 * kept.size, transcendentals=0),
        name="join_back",
    )(query, kept, landed, cos, ahead, behind)


def stack_heads(block, group, per):
    return jnp.concatenate(
        [block[:, (group * per + h) * HD : (group * per + h + 1) * HD] for h in range(per)],
        axis=0,
    )


def key_block(own_ref, other_ref, at, column):
    return jnp.concatenate(
        [own_ref[at, :, column : column + HD], other_ref[at, :, column : column + HD]],
        axis=0,
    )


def key_limits(meta_ref, slots_ref, local):
    me, length = meta_ref[0], meta_ref[1 + pl.program_id(0)]
    pair = 2 * local
    full = lax.div(jnp.minimum(me * local + 1, length), pair)
    some = lax.div(jnp.minimum((me + 1) * local, length) + pair - 1, pair)
    limit = jnp.minimum(slots_ref[...], length - 1)
    row = lax.broadcasted_iota(jnp.int32, (pair, 1), 0)
    core = lax.rem(me, 2)
    within = jnp.where(row < local, core * local + row, (1 - core) * local + row - local)
    return me, length, full, some, limit, within


def keep_allowed(scores, base, within, limit, slots, window):
    place = base + within
    allowed = place <= limit
    if window:
        allowed = allowed & (slots - place < WINDOW)
    return jnp.where(allowed, scores, NEGATIVE)


def attend_kernel(meta_ref, slots_ref, query_ref, own_ref, other_ref, att_ref, lse_ref, stacked, total, *, groups, per, window):
    local = query_ref.shape[0]
    pair = 2 * local
    kv_cols = groups * HD
    me, _, full, some, limit, within = key_limits(meta_ref, slots_ref, local)
    if window:
        full = full * 0
    factor = HD ** (-0.5) * LOG2E
    for g in range(groups):
        stacked[g] = stack_heads(query_ref[...], g, per)
        total[g] = jnp.zeros(total.shape[1:], jnp.float32)

    def step(m, carry, masked):
        at = jnp.bitwise_xor(m, lax.div(me, 2))
        out = []
        for g in range(groups):
            top, weight = carry[g]
            keys = key_block(own_ref, other_ref, at, g * HD)
            values = key_block(own_ref, other_ref, at, kv_cols + g * HD)
            scores = dot(keys, stacked[g], 1, 1) * factor
            if masked:
                scores = keep_allowed(scores, m * pair, within, limit, slots_ref[...], window)
            higher = jnp.maximum(top, jnp.max(scores, axis=0, keepdims=True))
            probs = jnp.exp2(scores - higher)
            shrink = jnp.exp2(top - higher)
            total[g] = total[g] * shrink + dot(values, probs.astype(LOW), 0, 0)
            out.append(
                (higher, weight * shrink + jnp.sum(probs, axis=0, keepdims=True))
            )
        return tuple(out)

    row = (1, per * local)
    carry = tuple(
        (jnp.full(row, NEGATIVE, jnp.float32), jnp.zeros(row, jnp.float32))
        for _ in range(groups)
    )
    carry = lax.fori_loop(0, full, lambda m, c: step(m, c, False), carry)
    carry = lax.fori_loop(full, some, lambda m, c: step(m, c, True), carry)
    for g in range(groups):
        top, weight = carry[g]
        lse_ref[0, g : g + 1, :] = top + jnp.log2(weight)
        out = (total[g] / weight).T.astype(LOW)
        for h in range(per):
            at = (g * per + h) * HD
            att_ref[:, at : at + HD] = out[h * local : (h + 1) * local]


def attend_back_kernel(
    meta_ref, slots_ref, cos_ref, sin_ref, query_ref, own_ref, other_ref, att_ref, grad_ref, lse_ref,
    grad_query_ref, grad_own_ref, grad_other_ref, stacked, stacked_grad, total, row_dot, *, groups, per, window,
):
    local = query_ref.shape[0]
    pair = 2 * local
    kv_cols = groups * HD
    me, length, full, some, limit, within = key_limits(meta_ref, slots_ref, local)
    if window:
        full = full * 0
    scale = HD ** (-0.5)
    live = me * local < length
    full = jnp.where(live, full, 0)
    some = jnp.where(live, some, 0)
    chips = own_ref.shape[0]
    chip = lax.div(me, 2)

    for g in range(groups):
        stacked[g] = stack_heads(query_ref[...], g, per)
        grads = stack_heads(grad_ref[...], g, per)
        stacked_grad[g] = grads
        product = grads.astype(jnp.float32) * stack_heads(att_ref[...], g, per).astype(jnp.float32)
        row_dot[g : g + 1, :] = jnp.sum(product.T, axis=0, keepdims=True)
        total[g] = jnp.zeros(total.shape[1:], jnp.float32)

    def clear(m, carry):
        at = jnp.bitwise_xor(m, chip)
        grad_own_ref[at] = jnp.zeros(grad_own_ref.shape[1:], LOW)
        grad_other_ref[at] = jnp.zeros(grad_other_ref.shape[1:], LOW)
        return carry

    def step(m, carry, masked):
        at = jnp.bitwise_xor(m, chip)
        for g in range(groups):
            keys = key_block(own_ref, other_ref, at, g * HD)
            values = key_block(own_ref, other_ref, at, kv_cols + g * HD)
            scores = dot(keys, stacked[g], 1, 1) * (scale * LOG2E)
            if masked:
                scores = keep_allowed(scores, m * pair, within, limit, slots_ref[...], window)
            probs = jnp.exp2(scores - lse_ref[0, g : g + 1, :])
            grad_probs = dot(values, stacked_grad[g], 1, 1)
            grad_scores = (probs * (grad_probs - row_dot[g : g + 1, :])).astype(LOW)
            grad_values = dot(probs.astype(LOW), stacked_grad[g], 1, 0).astype(LOW)
            grad_keys = (dot(grad_scores, stacked[g], 1, 0) * scale).astype(LOW)
            total[g] += dot(keys, grad_scores, 0, 0)
            for column, grads in ((g * HD, grad_keys), (kv_cols + g * HD, grad_values)):
                grad_own_ref[at, :, column : column + HD] = grads[:local]
                grad_other_ref[at, :, column : column + HD] = grads[local:]
        return carry

    lax.fori_loop(0, full, lambda m, c: step(m, c, False), 0)
    lax.fori_loop(full, some, lambda m, c: step(m, c, True), 0)
    lax.fori_loop(some, chips, clear, 0)
    half = HD // 2
    cos, sin = cos_ref[...], sin_ref[...]
    for g in range(groups):
        grads = total[g] * scale
        first, second = grads[:half], grads[half:]
        turned = jnp.concatenate(
            [first * cos + second * sin, second * cos - first * sin], axis=0
        ).T.astype(LOW)
        for h in range(per):
            at = (g * per + h) * HD
            grad_query_ref[:, at : at + HD] = turned[h * local : (h + 1) * local]


def attention_specs(seqs, local, q_cols, kv_both, chips, groups, columns):
    meta = pl.BlockSpec(memory_space=pltpu.SMEM)
    whole = lambda shape: pl.BlockSpec(shape, lambda s: (0,) * len(shape))
    queries = pl.BlockSpec((local, q_cols), lambda s: (s, 0))
    keys = pl.BlockSpec((chips, local, kv_both), lambda s: (0, s, 0))
    lse = pl.BlockSpec((1, groups, columns), lambda s: (s, 0, 0))
    return meta, whole, queries, keys, lse


def attend(meta, slots, query, own, other, groups, window):
    seqs = meta.shape[0] - 1
    rows, q_cols = query.shape
    local = rows // seqs
    chips, _, kv_both = own.shape
    per = q_cols // HD // groups
    columns = per * local
    smem, whole, queries, keys, lse = attention_specs(
        seqs, local, q_cols, kv_both, chips, groups, columns
    )
    pairs = rows * q_cols // HD * 2 * chips * local
    return pl.pallas_call(
        functools.partial(attend_kernel, groups=groups, per=per, window=window),
        grid=(seqs,),
        in_specs=[smem, whole((1, columns)), queries, keys, keys],
        out_specs=[queries, lse],
        out_shape=[
            jax.ShapeDtypeStruct((rows, q_cols), LOW),
            jax.ShapeDtypeStruct((seqs, groups, columns), jnp.float32),
        ],
        scratch_shapes=[
            pltpu.VMEM((groups, columns, HD), LOW),
            pltpu.VMEM((groups, HD, columns), jnp.float32),
        ],
        compiler_params=pltpu.CompilerParams(vmem_limit_bytes=VMEM_LIMIT),
        cost_estimate=pl.CostEstimate(
            flops=12 * pairs * HD // COST, bytes_accessed=4 * own.size // COST, transcendentals=0
        ),
        name="attend",
    )(meta, slots, query, own, other)


def attend_back(meta, slots, cos, sin, query, own, other, att, grad, lse_rows, groups, window):
    seqs = meta.shape[0] - 1
    rows, q_cols = query.shape
    local = rows // seqs
    chips, _, kv_both = own.shape
    per = q_cols // HD // groups
    columns = per * local
    smem, whole, queries, keys, lse = attention_specs(
        seqs, local, q_cols, kv_both, chips, groups, columns
    )
    pairs = rows * q_cols // HD * 2 * chips * local
    return pl.pallas_call(
        functools.partial(attend_back_kernel, groups=groups, per=per, window=window),
        grid=(seqs,),
        in_specs=[
            smem, whole((1, columns)), whole(cos.shape), whole(cos.shape),
            queries, keys, keys, queries, queries, lse,
        ],
        out_specs=[queries, keys, keys],
        out_shape=[
            jax.ShapeDtypeStruct((rows, q_cols), LOW),
            jax.ShapeDtypeStruct(own.shape, LOW),
            jax.ShapeDtypeStruct(own.shape, LOW),
        ],
        scratch_shapes=[
            pltpu.VMEM((groups, columns, HD), LOW),
            pltpu.VMEM((groups, columns, HD), LOW),
            pltpu.VMEM((groups, HD, columns), jnp.float32),
            pltpu.VMEM((groups, columns), jnp.float32),
        ],
        compiler_params=pltpu.CompilerParams(vmem_limit_bytes=VMEM_LIMIT),
        cost_estimate=pl.CostEstimate(
            flops=30 * pairs * HD // COST, bytes_accessed=8 * own.size // COST, transcendentals=0
        ),
        name="attend_back",
    )(meta, slots, cos, sin, query, own, other, att, grad, lse_rows)


def take_chunk(rows, index, size):
    return lax.dynamic_slice_in_dim(rows, index * size, size, axis=0)


def norm_scale(values):
    return lax.rsqrt(jnp.mean(values * values, axis=-1, keepdims=True) + EPSILON)


def norm_back(grad, gain, normed, scale):
    scaled = grad * gain
    return scale * (scaled - normed * jnp.mean(scaled * normed, axis=-1, keepdims=True))


def per_device(
    tokens,
    lengths,
    cotangent,
    attn_gain,
    query_weight,
    key_weight,
    value_weight,
    out_weight,
    ffn_gain,
    gate_weight,
    up_weight,
    down_weight,
):
    micro_count, seq_count, local_tokens, width = tokens.shape
    place = line_place(lax.axis_index("head"))
    me = lax.axis_index("ctx")
    lines = lax.axis_size("head")
    q_cols = query_weight.shape[1]
    kv_cols = key_weight.shape[1]
    used = q_cols + 2 * kv_cols
    padded = (used + 2 + 127) // 128 * 128

    qkv_shard = jnp.concatenate(
        [
            query_weight,
            key_weight,
            value_weight,
            attn_gain[:, None],
            ffn_gain[:, None],
            jnp.zeros((query_weight.shape[0], padded - used - 2), LOW),
        ],
        axis=1,
    )
    full_qkv = lax.all_gather(qkv_shard, "ctx", axis=0, tiled=True)
    full_out = lax.all_gather(out_weight.T, "ctx", axis=0, tiled=True)
    full_gate = lax.all_gather(gate_weight, "ctx", axis=0, tiled=True)
    full_up = lax.all_gather(up_weight, "ctx", axis=0, tiled=True)
    full_down = lax.all_gather(down_weight.T, "ctx", axis=0, tiled=True)
    gains = full_qkv[:, used : used + 2].T.astype(jnp.float32)
    gain_attn = gains[0:1]
    gain_ffn = gains[1:2]

    heads = q_cols // HD
    groups = kv_cols // HD
    per = heads // groups
    span_total = local_tokens * lax.axis_size("ctx")
    window = span_total > WINDOW
    query_slots = me * local_tokens + jnp.arange(local_tokens, dtype=jnp.int32)
    cosine, sine = angles(query_slots)
    piece_rows = seq_count * local_tokens
    rows = micro_count * piece_rows
    chunk = piece_rows // lines
    pieces = range(micro_count)

    nothing = jnp.zeros_like(sine)
    turning = heads + groups
    rest = padded - turning * HD
    cos_wide = jnp.concatenate(
        [cosine] * (2 * turning) + [jnp.ones((local_tokens, rest), jnp.float32)], axis=1
    )
    ahead = jnp.concatenate(
        [-sine, nothing] * turning + [jnp.zeros((local_tokens, rest), jnp.float32)], axis=1
    )
    behind = jnp.concatenate(
        [nothing, sine] * turning + [jnp.zeros((local_tokens, rest), jnp.float32)], axis=1
    )
    both = 2 * kv_cols
    rest = (both + 127) // 128 * 128 - groups * HD
    key_tables = (
        jnp.concatenate(
            [cosine] * (2 * groups) + [jnp.ones((local_tokens, rest), jnp.float32)], axis=1
        ),
        jnp.concatenate(
            [-sine, nothing] * groups + [jnp.zeros((local_tokens, rest), jnp.float32)], axis=1
        ),
        jnp.concatenate(
            [nothing, sine] * groups + [jnp.zeros((local_tokens, rest), jnp.float32)], axis=1
        ),
    )
    cos_tall = jnp.concatenate([cosine.T] * per, axis=1)
    sin_tall = jnp.concatenate([sine.T] * per, axis=1)
    slots = jnp.concatenate([query_slots] * per)[None]

    flat = tokens.reshape(rows, width)
    input_one, query_rot, kv = project(
        flat, gain_attn, full_qkv, cos_wide, ahead, behind, micro_count, q_cols, 2 * kv_cols
    )

    def piece_of(array, piece):
        return array[piece * piece_rows : (piece + 1) * piece_rows]

    live = (query_slots[None, None, :] < lengths[:, :, None]).reshape(rows, 1)
    grad_out = jnp.where(live, cotangent.reshape(rows, width), 0)

    metas = [
        jnp.concatenate([me.astype(jnp.int32)[None], lengths[piece]]) for piece in pieces
    ]
    bits = chip_bits()
    keys = [
        cube_gather(piece_of(kv, piece), bits if piece % 2 == 0 else bits[::-1])
        for piece in pieces
    ]

    def attend_piece(piece, *others):
        own, other = keys[piece]
        query = after(piece_of(query_rot, piece), *others)
        att, lse = attend(metas[piece], slots, query, own, other, groups, window)
        return att, lse, dot(att, full_out, 1, 1).astype(LOW)

    def residual(piece, summed):
        piece_tokens = take_chunk(piece_of(flat, piece), place, chunk).astype(jnp.float32)
        hidden = piece_tokens + summed
        scale = norm_scale(hidden)
        normed = hidden * scale
        return hidden, scale, normed, (normed * gain_ffn).astype(LOW)

    def hidden_back(piece, grad_two, kept):
        _, scale, normed, _ = kept
        gain_term = jnp.sum(grad_two * normed, axis=0)
        grad_hidden = take_chunk(piece_of(grad_out, piece), place, chunk).astype(
            jnp.float32
        ) + norm_back(grad_two, gain_ffn, normed, scale)
        return gain_term, grad_hidden, grad_hidden.astype(LOW)

    def scatter_weight(term):
        return lax.psum_scatter(term, "ctx", scatter_dimension=0, tiled=True)

    def weight_grad(left, right, *others):
        term = dot(after(left, *others), right, 0, 0).astype(LOW)
        return with_layout_constraint(term, Layout((0, 1)))

    def attention_back(piece, grad_low, *others):
        grad_att = dot(after(grad_low, *others), full_out, 1, 0).astype(LOW)
        own, other = keys[piece]
        return attend_back(
            metas[piece], slots, cos_tall, sin_tall, piece_of(query_rot, piece), own, other,
            atts[piece], grad_att, lses[piece], groups, window,
        )

    def one_back(back, *others):
        return dot(after(back, *others), full_qkv[:, :used], 1, 1).astype(LOW)

    def tokens_back(piece, grad_one, grad_hidden):
        piece_tokens = take_chunk(piece_of(flat, piece), place, chunk).astype(jnp.float32)
        scale = norm_scale(piece_tokens)
        normed = piece_tokens * scale
        gain_term = jnp.sum(grad_one * normed, axis=0)
        total = grad_hidden + norm_back(grad_one, gain_attn, normed, scale)
        return gain_term, total.astype(LOW)

    att0, lse0, branch0 = attend_piece(0)
    sum0 = ChainScatter(branch0)
    sum0.next()
    att1, lse1, branch1 = attend_piece(1, branch0)
    atts, lses = (att0, att1), (lse0, lse1)
    sum1 = ChainScatter(branch1, *sum0.landed)
    kept0 = residual(0, sum0.finish())
    two0 = ChainGather(kept0[3])
    sum1.next()
    two0.next()
    two0.next(full_gate, full_up)
    kept1 = residual(1, sum1.finish())
    two1 = Gather(kept1[3])
    input0 = two0.finish()

    act0, grad_gate0, grad_up0 = feed(
        after(input0, kept1[3]), piece_of(grad_out, 0), full_gate, full_up, full_down
    )
    two1.next(full_down)
    back_two0 = back_through((after(grad_gate0, two1.landed), grad_up0), (full_gate, full_up))
    back_sum0 = Scatter(back_two0)
    input1 = two1.finish()
    act1, grad_gate1, grad_up1 = feed(
        after(input1, back_two0), piece_of(grad_out, 1), full_gate, full_up, full_down
    )
    back_sum0.next(act1)
    acts = jnp.concatenate([act0, act1], axis=0)
    down_term = weight_grad(grad_out, acts, back_sum0.kept)
    down_grad = scatter_weight(down_term)
    back_two1 = back_through((after(grad_gate1, down_term), grad_up1), (full_gate, full_up))
    gain0, grad_hidden0, low0 = hidden_back(0, back_sum0.finish(back_two1), kept0)
    hidden0 = Gather(low0)
    back_sum1 = Scatter(back_two1)
    ffn = back_through((after(acts, low0, back_two1),), (full_down,))
    input_two = jnp.concatenate([input0, input1], axis=0)
    gate_term = weight_grad(
        input_two,
        jnp.concatenate([grad_gate0, grad_gate1], axis=0),
        ffn,
        back_sum1.landed,
        hidden0.landed,
    )
    gate_grad = scatter_weight(gate_term)
    hidden0.next()
    back_sum1.next()
    up_term = weight_grad(
        input_two, jnp.concatenate([grad_up0, grad_up1], axis=0), gate_term
    )
    up_grad = scatter_weight(up_term)
    whole0 = hidden0.finish(up_term)
    mixed0 = Scatter(piece_of(ffn, 0), whole0)
    gain1, grad_hidden1, low1 = hidden_back(1, back_sum1.finish(up_term), kept1)
    hidden1 = ChainGather(low1)
    query0, own0, other0 = attention_back(0, whole0, low1)
    keys0 = Reduce(own0, other0, bits)
    hidden1.next()
    keys0.next(mixed0.landed)
    mixed0.next()
    whole1 = hidden1.finish()
    mixed1 = Scatter(piece_of(ffn, 1), whole1)
    whole_mixed0 = ChainGather((kept0[0] + mixed0.finish()).astype(LOW))
    query1, own1, other1 = attention_back(
        1, whole1, query0, keys0.sent, mixed1.held
    )
    keys1 = Reduce(own1, other1, bits)
    keys0.next(mixed1.landed)
    mixed1.next()
    whole_mixed0.next()
    keys1.next()
    back0 = join_back(query0, *keys0.finish(), *key_tables)
    back_one0 = one_back(back0, query1, keys1.sent)
    one0 = Scatter(back_one0)
    whole_mixed1 = ChainGather((kept1[0] + mixed1.finish()).astype(LOW))
    keys1.next()
    back1 = join_back(query1, *keys1.finish(), *key_tables)
    back_one1 = one_back(back1, back_one0, one0.held)
    one1 = Scatter(back_one1)
    one0.next()
    whole_mixed1.next()
    last_term = jnp.concatenate(
        [
            weight_grad(
                input_one, jnp.concatenate([back0, back1], axis=0), back_one1, gate_grad
            ),
            weight_grad(
                jnp.concatenate([whole0, whole1], axis=0),
                jnp.concatenate([att0, att1], axis=0),
                back_one1,
            ),
        ],
        axis=1,
    )
    last_grad = scatter_weight(last_term).astype(jnp.float32)
    qkv_grad, out_grad = last_grad[:, :used], last_grad[:, used:]
    gain2, total0 = tokens_back(0, one0.finish(), grad_hidden0)
    tokens0 = ChainGather(total0)
    tokens0_first = tokens0.landed
    one1.next()
    tokens0.next()
    gain3, total1 = tokens_back(1, one1.finish(tokens0_first), grad_hidden1)
    tokens1 = ChainGather(total1)
    gain_terms = after(jnp.stack([gain2 + gain3, gain0 + gain1]), total1)
    for bit in line_bits():
        gain_terms = gain_terms + line_swap(gain_terms, bit)
    gain_terms = jnp.swapaxes(
        gain_terms.reshape(2, lax.axis_size("ctx"), attn_gain.shape[0]), 0, 1
    )
    for bit in (bits[::-1] + [1]):
        half = gain_terms.shape[0] // 2
        mine = lax.rem(me // bit, 2)
        got = lax.ppermute(take_chunk(gain_terms, 1 - mine, half), "ctx", flip(bit))
        gain_terms = take_chunk(gain_terms, mine, half) + got
    gain_terms = gain_terms[0]
    gate_out = gate_grad.astype(jnp.float32)
    up_out = up_grad.astype(jnp.float32)
    down_out = down_grad.T.astype(jnp.float32)
    tokens1.next(gain_terms)
    mixed = jnp.stack([whole_mixed0.finish(), whole_mixed1.finish()], axis=0).reshape(tokens.shape)
    token_grad = (
        jnp.stack([tokens0.finish(), tokens1.finish(gate_out, up_out, down_out)], axis=0)
        .reshape(tokens.shape)
        .astype(jnp.float32)
    )
    return (
        mixed,
        token_grad,
        gain_terms[0],
        qkv_grad[:, :q_cols],
        qkv_grad[:, q_cols : q_cols + kv_cols],
        qkv_grad[:, q_cols + kv_cols :],
        out_grad.T,
        gain_terms[1],
        gate_out,
        up_out,
        down_out,
    )


def solution(mesh):
    placed = (
        P(None, None, "ctx", None),
        P(),
        P(None, None, "ctx", None),
        P("ctx"),
        P("ctx", "head"),
        P("ctx", "head"),
        P("ctx", "head"),
        P("head", "ctx"),
        P("ctx"),
        P("ctx", "head"),
        P("ctx", "head"),
        P("head", "ctx"),
    )
    return jax.shard_map(
        per_device,
        mesh=mesh,
        in_specs=placed,
        out_specs=(
            P(None, None, "ctx", None),
            P(None, None, "ctx", None),
            P("ctx"),
            P("ctx", "head"),
            P("ctx", "head"),
            P("ctx", "head"),
            P("head", "ctx"),
            P("ctx"),
            P("ctx", "head"),
            P("ctx", "head"),
            P("head", "ctx"),
        ),
        check_vma=False,
    )
```
